32 devices in a mesh: row: 4 (over y, x), col: 8 (over z, core).
Axes of the slice: x: 2, y: 2, z: 4, core: 2. Of those that a mesh axis runs over, the one named last changes fastest.
Arguments:
- a_blocks: bfloat16 [8, 128, 128, 128], P('col', 'row'), may hold values from -0.5 to 0.5
- a_rows: int32 [8, 128], P('col', 'row'), may hold values from 0 to 7, as said below
- b_blocks: bfloat16 [4, 128, 128, 128], P('row', 'col'), may hold values from -6 to 6
- b_cols: int32 [4, 128], P('row', 'col'), may hold values from 0 to 15, as said below
- c_keep: int32 [4, 8, 24], P('row', 'col'), may hold values from 0 to 127, as said below
- c_owner: int32 [4, 8, 24], P('row', 'col'), may hold values from 0 to 31, as said below
- c_slot: int32 [4, 8, 24], P('row', 'col'), may hold values from 0 to 63, as said below
Outputs:
- owned_blocks: bfloat16 [4, 512, 128, 128], P('row', 'col')
The draws below stay inside these ranges and needn't reach their ends.
Inputs may be any that keep to these rules, and one draw needn't show every extreme that they name: `a_rows`: for each j, i and block column c of the panel, the slots c * (2) to (c + 1) * 2 - 1 name 2 distinct rows. `b_cols`: for each i, j and block row of the half panel, its 2 consecutive slots name distinct columns. `c_keep`: the 24 positions of one device are distinct. `c_owner`: each device sends to exactly 12 distinct owners, exactly 2 blocks to each; some owner receives 64 blocks in all, none more. `c_slot`: the pairs (owner, slot) are distinct over all kept blocks of all devices.
All inputs are finite; a program needn't handle non-finite values.
Results may differ from the reference program's by a relative error of at most 0.001.
Values may be sent and summed in bfloat16 or wider, within the bound.
No kernel may reach another device: no remote copies, remote signals or barrier semaphores. Data moves between devices by JAX's collectives and lax.ppermute only.
A program may use at most 128 MiB of HBM per device.

```python
import jax
import jax.numpy as jnp
import numpy as np
from jax import lax

BS = 128
RB = 8
CB = 16
SA = 32
SBH = 16
FANOUT = 12
KC = 24
RCAP = 64
N_ROW = 4
N_COL = 8
DEVICES = 32


def owner_plan(key):
    counts = np.concatenate([np.full(DEVICES // 8, DEVICES), np.full(DEVICES // 8, DEVICES // 2), np.full(3 * DEVICES // 4, DEVICES // 4)])
    rank_of = np.repeat(np.arange(DEVICES), counts)
    starts = np.concatenate([np.zeros(1, np.int64), np.cumsum(counts)[:-1]])
    positions = np.arange(DEVICES * FANOUT)
    offsets = positions - starts[rank_of]
    key_owner, key_source, key_slot, key_shuffle = jax.random.split(key, 4)
    owner_label = jax.random.permutation(key_owner, DEVICES).astype(jnp.int32)
    source_label = jax.random.permutation(key_source, DEVICES).astype(jnp.int32)

    def slot_order(subkey):
        return jax.random.permutation(subkey, RCAP).astype(jnp.int32)

    def kept_order(subkey):
        return jax.random.permutation(subkey, KC).astype(jnp.int32)
    slot_table = jax.vmap(slot_order)(jax.random.split(key_slot, DEVICES))
    owners = owner_label[rank_of]
    sources = source_label[positions % DEVICES]
    rounds = positions // DEVICES
    owner_grid = jnp.zeros((DEVICES, KC), jnp.int32)
    slot_grid = jnp.zeros((DEVICES, KC), jnp.int32)
    for member in range(2):
        owner_grid = owner_grid.at[sources, 2 * rounds + member].set(owners)
        slot_grid = slot_grid.at[sources, 2 * rounds + member].set(slot_table[owners, 2 * offsets + member])
    shuffle = jax.vmap(kept_order)(jax.random.split(key_shuffle, DEVICES))
    owner_grid = jnp.take_along_axis(owner_grid, shuffle, axis=1)
    slot_grid = jnp.take_along_axis(slot_grid, shuffle, axis=1)
    return (owner_grid.reshape(N_ROW, N_COL, KC), slot_grid.reshape(N_ROW, N_COL, KC))


def draw_a_rows(key, part):
    key = jax.random.fold_in(key, 11)

    def pick_rows(subkey):
        return jax.random.permutation(subkey, RB)[:RB // 4].astype(jnp.int32)
    chosen = jax.vmap(pick_rows)(jax.random.split(key, N_COL * N_ROW * CB))
    return chosen.reshape(N_COL, N_ROW * SA)


def draw_b_cols(key, part):
    key = jax.random.fold_in(key, 13)

    def pick_cols(subkey):
        return jax.random.permutation(subkey, CB)[:CB // 8].astype(jnp.int32)
    chosen = jax.vmap(pick_cols)(jax.random.split(key, N_ROW * N_COL * (CB // 2)))
    return chosen.reshape(N_ROW, N_COL * SBH)


def draw_c_keep(key, part):
    key = jax.random.fold_in(key, 17)

    def pick_kept(subkey):
        return jax.random.permutation(subkey, RB * CB)[:KC].astype(jnp.int32)
    chosen = jax.vmap(pick_kept)(jax.random.split(key, DEVICES))
    return chosen.reshape(N_ROW, N_COL, KC)


def draw_c_owner(key, part):
    plan = owner_plan(key)
    return plan[0]


def draw_c_slot(key, part):
    plan = owner_plan(key)
    return plan[1]


def shard_levels(rng, extent, pieces, smallest, top_value):
    gain = 1.0
    for dim, blocks in pieces:
        draws = jax.random.uniform(jax.random.fold_in(jax.random.fold_in(rng, 6), dim), (blocks,), jnp.float32, smallest / len(pieces), top_value / len(pieces))
        gain = gain * jnp.repeat(jnp.exp(draws), extent[dim] // blocks).reshape((-1,) + (1,) * (len(extent) - 1 - dim))
    return gain


def bell_draw(key, shape, scale, most, pieces=(), kind=jnp.bfloat16):
    level = shard_levels(key, shape, pieces, -0.22, 0.18) if pieces else 1.0
    result = jax.random.normal(key, shape, jnp.float32) * scale * level
    return jnp.minimum(jnp.maximum(result, -most), most).astype(kind)


def setup_inputs(seed: int = 0) -> dict:
    key_of = jax.random.split(jax.random.key(seed), 8)
    a_blocks = bell_draw(key_of[0], (N_COL, N_ROW * SA, BS, BS), BS ** -0.5, 0.5, ((0, 8), (1, 4)))
    a_rows = draw_a_rows(jax.random.fold_in(key_of[7], 71), 0)
    b_blocks = bell_draw(key_of[2], (N_ROW, N_COL * SBH, BS, BS), 1.0, 6.0, ((0, 4), (1, 8)))
    b_cols = draw_b_cols(jax.random.fold_in(key_of[7], 71), 0)
    c_keep = draw_c_keep(jax.random.fold_in(key_of[7], 71), 0)
    c_owner = draw_c_owner(jax.random.fold_in(key_of[7], 71), 0)
    c_slot = draw_c_slot(jax.random.fold_in(key_of[7], 71), 0)
    return dict(a_blocks=a_blocks, a_rows=a_rows, b_blocks=b_blocks, b_cols=b_cols, c_keep=c_keep, c_owner=c_owner, c_slot=c_slot)


def region_products(a_panel, row_ids, b_panel, col_ids, panel_width, region_size):
    block_size = a_panel.shape[-1]
    left_blocks = a_panel.reshape(panel_width, -1, block_size, block_size).astype(jnp.float32)
    right_blocks = b_panel.reshape(panel_width, -1, block_size, block_size).astype(jnp.float32)
    products = jnp.einsum("kaxy,kbyz->kabxz", left_blocks, right_blocks)
    targets = row_ids.reshape(panel_width, -1)[:, :, None] * panel_width + col_ids.reshape(panel_width, -1)[:, None, :]
    return jax.ops.segment_sum(products.reshape(-1, block_size, block_size), targets.reshape(-1).astype(jnp.int32), num_segments=region_size)


def reference(a_blocks, a_rows, b_blocks, b_cols, c_keep, c_owner, c_slot):
    device_count = N_ROW * N_COL

    def one_device(device_index):
        zero = jnp.zeros((), jnp.int32)
        grid_row = (device_index // N_COL).astype(jnp.int32)
        grid_col = (device_index % N_COL).astype(jnp.int32)
        accumulated = jnp.zeros((RB * CB, BS, BS), jnp.float32)
        for panel_index in range(N_ROW):
            a_source = ((panel_index - grid_col) % N_ROW).astype(jnp.int32)
            b_source = ((panel_index - grid_row) % N_ROW).astype(jnp.int32)
            a_start = (a_source * SA).astype(jnp.int32)
            b_first = (b_source * SBH).astype(jnp.int32)
            b_second = ((b_source + N_ROW) * SBH).astype(jnp.int32)
            a_panel = lax.dynamic_slice(a_blocks, (grid_col, a_start, zero, zero), (1, SA, BS, BS))[0]
            a_index = lax.dynamic_slice(a_rows, (grid_col, a_start), (1, SA))[0]
            first_half = lax.dynamic_slice(b_blocks, (grid_row, b_first, zero, zero), (1, SBH, BS, BS))[0]
            second_half = lax.dynamic_slice(b_blocks, (grid_row, b_second, zero, zero), (1, SBH, BS, BS))[0]
            first_cols = lax.dynamic_slice(b_cols, (grid_row, b_first), (1, SBH))[0]
            second_cols = lax.dynamic_slice(b_cols, (grid_row, b_second), (1, SBH))[0]
            b_panel = jnp.concatenate([first_half, second_half], axis=0)
            b_index = jnp.concatenate([first_cols, second_cols], axis=0)
            accumulated = accumulated + region_products(a_panel, a_index, b_panel, b_index, CB, RB * CB)
        keep_list = c_keep[grid_row, grid_col]
        return accumulated[keep_list].astype(jnp.bfloat16)

    kept_blocks = lax.map(one_device, jnp.arange(device_count, dtype=jnp.int32))
    targets = (c_owner * RCAP + c_slot).reshape(-1).astype(jnp.int32)
    owned_blocks = jnp.zeros((device_count * RCAP, BS, BS), kept_blocks.dtype)
    owned_blocks = owned_blocks.at[targets].set(kept_blocks.reshape(-1, BS, BS))
    return owned_blocks.reshape(N_ROW, N_COL * RCAP, BS, BS)
```

```python
import functools

import jax
import jax.numpy as jnp
from jax import lax
from jax.experimental import pallas as pl
from jax.experimental.pallas import tpu as pltpu
from jax.sharding import PartitionSpec as P

RB = 8
SCAP = 2
UNROLL = 8
CORES = 2
SIDE = 2
PARTS = 2
EXCHANGE_ROWS = 8
LANES = 128

SMEM = pl.BlockSpec(memory_space=pltpu.SMEM)
VMEM = pl.BlockSpec(memory_space=pltpu.VMEM)
HBM = pl.BlockSpec(memory_space=pltpu.HBM)
ANY = pl.BlockSpec(memory_space=pl.ANY)


def limit(megabytes):
    return pltpu.CompilerParams(vmem_limit_bytes=megabytes * 1024 * 1024)


def announce_kernel(told, ids, out_ref, pos, base, sent):
    kept_count = pos.shape[0]
    base[...] = jnp.zeros_like(base)
    base[pl.ds(0, 1), :] = jnp.full((1, LANES), SCAP * out_ref.shape[0], jnp.int32)
    base[pl.ds(1, 1), pl.ds(0, ids.shape[1])] = ids[...]
    out_ref[...] = jnp.broadcast_to(base[...][None], out_ref.shape)
    lane = lax.broadcasted_iota(jnp.int32, (1, LANES), 1)

    def clear(d, carry):
        sent[d] = 0
        return carry

    lax.fori_loop(0, out_ref.shape[0], clear, 0, unroll=8)

    def tell(q, carry):
        owner = told[q]
        order = sent[owner]
        pos[q] = owner * SCAP + order
        sent[owner] = order + 1
        out_ref[owner, pl.ds(0, 1), :] = jnp.where(lane == order, told[kept_count + q], out_ref[owner, pl.ds(0, 1), :])
        return carry

    lax.fori_loop(0, kept_count, tell, 0)


def announce(device_count, owners, slots, a_ids, b_ids):
    return pl.pallas_call(
        announce_kernel,
        out_shape=[
            pltpu.VMEM((device_count, EXCHANGE_ROWS, LANES), jnp.int32),
            jax.ShapeDtypeStruct(owners.shape, jnp.int32),
        ],
        in_specs=[SMEM, VMEM],
        out_specs=[VMEM, SMEM],
        scratch_shapes=[pltpu.VMEM((EXCHANGE_ROWS, LANES), jnp.int32), pltpu.SMEM((device_count,), jnp.int32)],
        compiler_params=limit(2),
        name="announce",
    )(jnp.concatenate([owners, slots]), jnp.concatenate([a_ids, b_ids], axis=1))


def choose_kernel(cuts, where, *refs):
    count = len(cuts)
    pairs = [(refs[2 * n], refs[2 * n + 1]) for n in range(count)]
    out_refs, sems = list(refs[2 * count + 1:-1]), refs[-1]
    core = where[1] % CORES
    waits = []
    for (first, second), parts in zip(pairs, cuts):
        size = first.shape[0] // parts
        for part in range(parts):
            out, sem, rows = out_refs[len(waits)], sems.at[len(waits)], pl.ds(part * size, size)
            pl.when(core == 0)(pltpu.make_async_copy(first.at[rows], out, sem).start)
            pl.when(core != 0)(pltpu.make_async_copy(second.at[rows], out, sem).start)
            waits.append(pltpu.make_async_copy(first.at[rows], out, sem))
    for copy in waits:
        copy.wait()


def choose(where, pairs, cuts, after):
    shapes = [
        pltpu.VMEM((first.shape[0] // parts, first.shape[1]), first.dtype)
        for (first, _), parts in zip(pairs, cuts)
        for _ in range(parts)
    ]
    return pl.pallas_call(
        functools.partial(choose_kernel, cuts),
        out_shape=shapes,
        in_specs=[SMEM] + [ANY] * (2 * len(pairs) + 1),
        out_specs=[VMEM] * len(shapes),
        scratch_shapes=[pltpu.SemaphoreType.DMA((len(shapes),))],
        compiler_params=limit(8),
        name="choose",
    )(where, *(piece for pair in pairs for piece in pair), after)


def tie_kernel(*refs):
    pass


def tied(array, after):
    return pl.pallas_call(
        tie_kernel,
        out_shape=jax.ShapeDtypeStruct(array.shape, array.dtype),
        in_specs=[ANY] * 2,
        out_specs=ANY,
        input_output_aliases={0: 0},
        compiler_params=limit(1),
        name="tied",
    )(array, after)


class Bringer:
    def __init__(self, a_ref, b_ref, sems, row_count, col_count):
        self.refs = {"a": (a_ref, a_ref.shape[0] // row_count), "b": (b_ref, b_ref.shape[0] // col_count)}
        self.sems, self.copies = sems, []

    def bring(self, which, ref, member, part=0, parts=1):
        target, size = self.refs[which]
        size //= parts
        rows = target.at[pl.ds(pl.multiple_of((member * parts + part) * size, size), size)]
        self.copies.append(pltpu.make_async_copy(ref, rows, self.sems.at[len(self.copies)]))
        self.copies[-1].start()

    def wait(self):
        for copy in self.copies:
            copy.wait()


def bring_chip(bringer, refs, shift, j, chips, parts=1):
    z, core = j // CORES, j % CORES
    for ref_core in (core, CORES - 1 - core):
        for part in range(parts):
            bringer.bring("b", refs.pop(0), (z - shift + chips) % chips * CORES + ref_core, part, parts)


def bring_first(bringer, refs, i, j, row_count, col_count):
    refs = list(refs)
    y_count, chips = row_count // SIDE, col_count // CORES
    y, x = i // SIDE, i % SIDE
    bringer.bring("a", refs.pop(0), i)
    bringer.bring("a", refs.pop(0), y * SIDE + SIDE - 1 - x)
    for shift in range(1, y_count):
        bringer.bring("a", refs.pop(0), (y - shift + y_count) % y_count * SIDE + x)
    for shift in (0, 1, chips - 1):
        bring_chip(bringer, refs, shift, j, chips)


def bring_rest(bringer, refs, i, j, row_count, col_count):
    refs = list(refs)
    y_count, chips = row_count // SIDE, col_count // CORES
    y, x = i // SIDE, i % SIDE
    for shift in range(1, y_count):
        bringer.bring("a", refs.pop(0), (y - shift + y_count) % y_count * SIDE + SIDE - 1 - x)
    for shift in range(2, chips // 2):
        bring_chip(bringer, refs, shift, j, chips)
        bring_chip(bringer, refs, chips - shift, j, chips)
    bring_chip(bringer, refs, chips // 2, j, chips, PARTS)


class Layout:
    def __init__(self, row_count, col_count, b_slots, kept_count):
        self.count = 2 * col_count * b_slots + UNROLL
        self.i, self.j = self.count + 1, self.count + 2
        self.pos = self.count + 3
        self.source = self.pos + kept_count
        self.size = self.source + SCAP * row_count * col_count + 1


def multiply_listed(listed, count, a_ref, b_ref, total):
    block = a_ref.shape[-1]

    def block_of(ref, index):
        return ref[pl.ds(pl.multiple_of(index * block, block), block), :]

    def multiply(step, carry):
        entries = [listed[step * UNROLL + u] for u in range(UNROLL)]
        products = [
            jnp.dot(
                block_of(a_ref, (entry >> 10) & 1023),
                block_of(b_ref, entry & 1023),
                preferred_element_type=jnp.float32,
            )
            for entry in entries
        ]
        for entry, product in zip(entries, products):
            q = entry >> 20
            total[q] = total[q] + product
        return carry

    lax.fori_loop(0, (count + UNROLL - 1) // UNROLL, multiply, 0)


def first_kernel(sizes, parts, keep, pos, where, exchange, *refs):
    row_count, col_count, b_slots = sizes
    pieces, refs = refs[:parts], refs[parts:]
    a_ref, b_ref, total, plan, ids, places, table, slot_rows, slot_table, listed, sems, sem = refs
    i, j = where[0], where[1]
    kept_count = keep.shape[0]
    panel_width = RB * col_count // row_count
    chips = col_count // CORES
    capacity = SCAP * row_count * col_count
    layout = Layout(row_count, col_count, b_slots, kept_count)
    bringer = Bringer(a_ref, b_ref, sems, row_count, col_count)
    bring_first(bringer, pieces, i, j, row_count, col_count)

    slot_rows[...] = exchange[:, 0, :]
    to_slot_table = pltpu.make_async_copy(slot_rows, slot_table, sem.at[0])
    to_slot_table.start()

    halves = col_count // row_count
    for half_panel in range(col_count):
        member, half = half_panel // halves, half_panel % halves
        rows = exchange[member * col_count + j, pl.ds(1, 1), :]
        ids[pl.ds(half_panel, 1), :] = rows if half == 0 else pltpu.roll(rows, LANES - half * b_slots, 1)
        source = half * row_count + (member + j - i + row_count) % row_count
        cols = exchange[i * col_count + source, pl.ds(1, 1), :]
        ids[pl.ds(col_count + half_panel, 1), :] = pltpu.roll(cols, LANES - halves * b_slots, 1)
    rows = ids[pl.ds(0, col_count), :] * panel_width
    cols = ids[pl.ds(col_count, col_count), :]
    even = lax.broadcasted_iota(jnp.int32, cols.shape, 1) % 2 == 0
    crossed = jnp.where(even, pltpu.roll(cols, LANES - 1, 1), pltpu.roll(cols, 1, 1))
    for cross, columns in enumerate([cols, crossed]):
        target = rows + columns
        found = jnp.full_like(target, kept_count)
        for q in range(kept_count):
            found = jnp.where(target == keep[q], q, found)
        places[pl.ds(cross * col_count, col_count), :] = found
    to_table = pltpu.make_async_copy(places, table, sem.at[1])
    to_table.start()
    total[...] = jnp.zeros_like(total)
    to_table.wait()

    def look(half_panel, counts):
        member = half_panel // halves
        source = (half_panel % halves) * row_count + (member + j - i + row_count) % row_count
        a_near = (member % SIDE == i % SIDE) | (member // SIDE == i // SIDE)
        apart = jnp.abs(j // CORES - source // CORES)
        b_near = (apart <= 1) | (apart == chips - 1)

        def scan(into, n):
            for slot in range(b_slots):
                for cross in range(2):
                    q = table[cross * col_count + half_panel, slot]
                    into[n] = (q << 20) | ((half_panel * b_slots + slot) << 10) | (source * b_slots + (slot ^ cross))
                    n = n + (q < kept_count).astype(jnp.int32)
            return n

        return lax.cond(
            a_near & b_near,
            lambda near, far: (scan(listed, near), far),
            lambda near, far: (near, scan(plan, far)),
            *counts,
        )

    near, far = lax.fori_loop(0, col_count, look, (jnp.int32(0), jnp.int32(0)))
    for extra in range(UNROLL):
        listed[near + extra] = kept_count << 20
        plan[far + extra] = kept_count << 20
    plan[layout.count], plan[layout.i], plan[layout.j] = far, i, j
    for q in range(kept_count):
        plan[layout.pos + q] = pos[q]

    def clear(s, carry):
        plan[layout.source + s] = -1
        return carry

    lax.fori_loop(0, capacity + 1, clear, 0, unroll=5)
    to_slot_table.wait()

    def mark(d, carry):
        for m in range(SCAP):
            plan[layout.source + slot_table[d, m]] = d * SCAP + m
        return carry

    lax.fori_loop(0, row_count * col_count, mark, 0, unroll=8)
    bringer.wait()
    multiply_listed(listed, near, a_ref, b_ref, total)


def first_products(sizes, keep, pos, where, exchange, pieces):
    row_count, col_count, b_slots = sizes
    block, kept_count = pieces[0].shape[-1], keep.shape[0]
    rows = col_count * b_slots * block
    return pl.pallas_call(
        functools.partial(first_kernel, sizes, len(pieces)),
        out_shape=[
            pltpu.VMEM((rows, block), jnp.bfloat16),
            pltpu.VMEM((rows, block), jnp.bfloat16),
            pltpu.VMEM((kept_count + 1, block, block), jnp.float32),
            jax.ShapeDtypeStruct((Layout(row_count, col_count, b_slots, kept_count).size,), jnp.int32),
        ],
        in_specs=[SMEM] * 3 + [VMEM] + [ANY] * len(pieces),
        out_specs=[VMEM] * 3 + [SMEM],
        scratch_shapes=[
            pltpu.VMEM((2 * col_count, LANES), jnp.int32),
            pltpu.VMEM((2 * col_count, LANES), jnp.int32),
            pltpu.SMEM((2 * col_count, LANES), jnp.int32),
            pltpu.VMEM((row_count * col_count, LANES), jnp.int32),
            pltpu.SMEM((row_count * col_count, LANES), jnp.int32),
            pltpu.SMEM((2 * col_count * b_slots + UNROLL,), jnp.int32),
            pltpu.SemaphoreType.DMA((len(pieces),)),
            pltpu.SemaphoreType.DMA((2,)),
        ],
        compiler_params=limit(26),
        cost_estimate=pl.CostEstimate(flops=5 * 10**9, bytes_accessed=0, transcendentals=0),
        name="first_products",
    )(keep, pos, where, exchange, *pieces)


def rest_kernel(sizes, parts, plan, *refs):
    row_count, col_count, b_slots = sizes
    pieces, refs = refs[3:3 + parts], refs[3 + parts:]
    a_ref, b_ref, total, send_ref, kept, sems, sem = refs
    kept_count = kept.shape[0]
    layout = Layout(row_count, col_count, b_slots, kept_count)
    bringer = Bringer(a_ref, b_ref, sems, row_count, col_count)
    bring_rest(bringer, pieces, plan[layout.i], plan[layout.j], row_count, col_count)
    bringer.wait()
    multiply_listed(plan, plan[layout.count], a_ref, b_ref, total)

    def finish(q, carry):
        kept[q] = total[q].astype(jnp.bfloat16)
        pltpu.make_async_copy(kept.at[q], send_ref.at[plan[layout.pos + q]], sem).start()
        return carry

    lax.fori_loop(0, kept_count, finish, 0, unroll=2)
    pltpu.make_async_copy(kept, kept, sem).wait()


def rest_products(sizes, kept_count, plan, buffers, pieces):
    row_count, col_count = sizes[:2]
    block = pieces[0].shape[-1]
    return pl.pallas_call(
        functools.partial(rest_kernel, sizes, len(pieces)),
        out_shape=[pltpu.VMEM(b.shape, b.dtype) for b in buffers]
        + [pltpu.HBM((SCAP * row_count * col_count, block, block), jnp.bfloat16)],
        in_specs=[SMEM] + [VMEM] * 3 + [ANY] * len(pieces),
        out_specs=[VMEM] * 3 + [HBM],
        scratch_shapes=[
            pltpu.VMEM((kept_count, block, block), jnp.bfloat16),
            pltpu.SemaphoreType.DMA((len(pieces),)),
            pltpu.SemaphoreType.DMA,
        ],
        input_output_aliases={1 + n: n for n in range(3)},
        compiler_params=limit(28),
        name="rest_products",
    )(plan, *buffers, *pieces)[-1]


def place_kernel(layout, plan, recv_ref, out_ref, zero, sem):
    zero[...] = jnp.zeros_like(zero)

    def place(s, carry):
        r = plan[layout.source + s]

        @pl.when(r >= 0)
        def _():
            pltpu.make_async_copy(recv_ref.at[r], out_ref.at[s], sem).start()

        @pl.when(r < 0)
        def _():
            pltpu.make_async_copy(zero, out_ref.at[s], sem).start()

        return carry

    lax.fori_loop(0, out_ref.shape[0], place, 0, unroll=4)
    pltpu.make_async_copy(recv_ref, out_ref, sem).wait()


def place(layout, plan, recv):
    block = recv.shape[-1]
    return pl.pallas_call(
        functools.partial(place_kernel, layout),
        out_shape=jax.ShapeDtypeStruct(recv.shape, recv.dtype),
        in_specs=[SMEM, VMEM],
        out_specs=HBM,
        scratch_shapes=[pltpu.VMEM((block, block), jnp.bfloat16), pltpu.SemaphoreType.DMA],
        compiler_params=limit(12),
        name="place",
    )(plan, recv)


def gathered(a_own, b_own, row_count, col_count, where, outgoing, multiply_near):
    chips, shifts = col_count // CORES, range(1, row_count // SIDE)

    def moved(piece, target):
        pairs = [(d, c, target(d, c)) for d in range(row_count) for c in range(col_count)]
        return lax.ppermute(
            piece, ("row", "col"), [(d * col_count + c, to[0] * col_count + to[1]) for d, c, to in pairs]
        )

    def around(d, c, by, other=False):
        core = CORES - 1 - c % CORES if other else c % CORES
        return d, (c // CORES + by) % chips * CORES + core

    def along(d, c, shift):
        return (d + shift * SIDE) % row_count, c

    def swapped(piece):
        return moved(piece, lambda d, c: around(d, c, 0, True))

    below = [moved(b_own, lambda d, c: around(d, c, 1))]
    above = [moved(b_own, lambda d, c: around(d, c, -1))]
    beside = moved(a_own, lambda d, c: (d ^ 1, c))
    ahead = [moved(a_own, lambda d, c, shift=shift: along(d, c, shift)) for shift in shifts]
    exchange = lax.all_to_all(outgoing, ("row", "col"), split_axis=0, concat_axis=0, tiled=True)
    for _ in range(2, chips // 2):
        below.append(moved(below[-1], lambda d, c: around(d, c, 1)))
        above.append(moved(above[-1], lambda d, c: around(d, c, -1)))
    pairs = [(below[-1], above[-1])] + [(piece, beside) for piece in ahead]
    cuts = [PARTS] + [1] * len(ahead)
    chosen = choose(where, pairs, cuts, exchange)
    passed, crossing = chosen[:PARTS], chosen[PARTS:]
    opposite = [moved(part, lambda d, c: around(d, c, 1 if c % CORES == 0 else -1)) for part in passed]
    diagonal = [
        moved(piece, lambda d, c, shift=shift: (d ^ 1, c) if c % CORES == 0 else along(d, c, shift))
        for shift, piece in zip(shifts, crossing)
    ]

    near = [a_own, beside, *ahead]
    for piece in (b_own, below[0], above[0]):
        near += [piece, swapped(piece)]
    *buffers, plan = multiply_near(exchange, near)
    opposite[-1] = tied(opposite[-1], plan)
    far = list(diagonal)
    for n in range(1, chips // 2 - 1):
        far += [below[n], swapped(below[n]), above[n], swapped(above[n])]
    return buffers, plan, far + opposite + [swapped(part) for part in opposite]


def body(a_blocks, a_rows, b_blocks, b_cols, c_keep, c_owner, c_slot):
    row_count = lax.axis_size("row")
    col_count = lax.axis_size("col")
    device_count = row_count * col_count
    block = a_blocks.shape[-1]
    keep, owner_ids, slot_ids = c_keep[0, 0], c_owner[0, 0], c_slot[0, 0]
    sizes = (row_count, col_count, b_cols.shape[1])
    where = jnp.stack([lax.axis_index("row"), lax.axis_index("col")]).astype(jnp.int32)

    outgoing, pos = announce(device_count, owner_ids, slot_ids, a_rows, b_cols)

    buffers, plan, far = gathered(
        a_blocks[0].reshape(-1, block),
        b_blocks[0].reshape(-1, block),
        row_count,
        col_count,
        where,
        outgoing,
        functools.partial(first_products, sizes, keep, pos, where),
    )
    send = rest_products(sizes, keep.shape[0], plan, buffers, far)
    recv = lax.all_to_all(send, ("row", "col"), split_axis=0, concat_axis=0, tiled=True)
    return place(Layout(*sizes, keep.shape[0]), plan, recv)[None]


def solution(mesh):
    return jax.shard_map(
        body,
        mesh=mesh,
        in_specs=(
            P("col", "row", None, None),
            P("col", "row"),
            P("row", "col", None, None),
            P("row", "col"),
            P("row", "col", None),
            P("row", "col", None),
            P("row", "col", None),
        ),
        out_specs=P("row", "col", None, None),
        check_vma=False,
    )
```

```python
import functools

import jax
import jax.numpy as jnp
from jax import lax
from jax.experimental import pallas as pl
from jax.experimental.pallas import tpu as pltpu
from jax.sharding import PartitionSpec as P

RB = 8
SCAP = 2
UNROLL = 8
CORES = 2
SIDE = 2
PARTS = 2
EXCHANGE_ROWS = 8
LANES = 128

SMEM = pl.BlockSpec(memory_space=pltpu.SMEM)
VMEM = pl.BlockSpec(memory_space=pltpu.VMEM)
HBM = pl.BlockSpec(memory_space=pltpu.HBM)
ANY = pl.BlockSpec(memory_space=pl.ANY)


def limit(megabytes):
    return pltpu.CompilerParams(vmem_limit_bytes=megabytes * 1024 * 1024)


def by_column(device, row_count, col_count):
    return device % col_count * row_count + device // col_count


def announce_kernel(
    row_count, col_count, owners_ref, slots_ref, a_ids_ref, b_ids_ref, out_ref, pos,
    base, sent, owners, slots, a_ids, b_ids, sems,
):
    moves = [(owners_ref, owners), (slots_ref, slots), (a_ids_ref, a_ids), (b_ids_ref, b_ids)]
    copies = [pltpu.make_async_copy(source, target, sems.at[n]) for n, (source, target) in enumerate(moves)]
    for copy in copies:
        copy.start()
    kept_count = pos.shape[0]
    base[...] = jnp.zeros_like(base)
    base[pl.ds(0, 1), :] = jnp.full((1, LANES), SCAP * out_ref.shape[0], jnp.int32)
    for copy in copies:
        copy.wait()
    base[pl.ds(1, 1), pl.ds(0, a_ids.shape[1])] = a_ids[...]
    base[pl.ds(2, 1), pl.ds(0, b_ids.shape[1])] = b_ids[...]
    out_ref[...] = jnp.broadcast_to(base[...][None], out_ref.shape)
    lane = lax.broadcasted_iota(jnp.int32, (1, LANES), 1)

    def clear(d, carry):
        sent[d] = 0
        return carry

    lax.fori_loop(0, out_ref.shape[0], clear, 0, unroll=8)

    def tell(q, carry):
        owner = owners[q]
        order = sent[owner]
        pos[q] = by_column(owner, row_count, col_count) * SCAP + order
        sent[owner] = order + 1
        out_ref[owner, pl.ds(0, 1), :] = jnp.where(lane == order, slots[q], out_ref[owner, pl.ds(0, 1), :])
        return carry

    lax.fori_loop(0, kept_count, tell, 0)


def announce(row_count, col_count, owners, slots, a_ids, b_ids):
    inputs = [pltpu.with_memory_space_constraint(array, pltpu.HBM) for array in (owners, slots, a_ids, b_ids)]
    return pl.pallas_call(
        functools.partial(announce_kernel, row_count, col_count),
        out_shape=[
            pltpu.VMEM((row_count * col_count, EXCHANGE_ROWS, LANES), jnp.int32),
            jax.ShapeDtypeStruct(owners.shape, jnp.int32),
        ],
        in_specs=[HBM] * 4,
        out_specs=[VMEM, SMEM],
        scratch_shapes=[
            pltpu.VMEM((EXCHANGE_ROWS, LANES), jnp.int32),
            pltpu.SMEM((row_count * col_count,), jnp.int32),
            pltpu.SMEM(owners.shape, jnp.int32),
            pltpu.SMEM(slots.shape, jnp.int32),
            pltpu.VMEM(a_ids.shape, jnp.int32),
            pltpu.VMEM(b_ids.shape, jnp.int32),
            pltpu.SemaphoreType.DMA((4,)),
        ],
        compiler_params=limit(2),
        name="announce",
    )(*inputs)


def choose_kernel(cuts, where, *refs):
    count = len(cuts)
    pairs = [(refs[2 * n], refs[2 * n + 1]) for n in range(count)]
    out_refs, sems = list(refs[2 * count + 1:-1]), refs[-1]
    core = where[1] % CORES
    waits = []
    for (first, second), parts in zip(pairs, cuts):
        size = first.shape[0] // parts
        for part in range(parts):
            out, sem, rows = out_refs[len(waits)], sems.at[len(waits)], pl.ds(part * size, size)
            pl.when(core == 0)(pltpu.make_async_copy(first.at[rows], out, sem).start)
            pl.when(core != 0)(pltpu.make_async_copy(second.at[rows], out, sem).start)
            waits.append(pltpu.make_async_copy(first.at[rows], out, sem))
    for copy in waits:
        copy.wait()


def choose(where, pairs, cuts, after):
    shapes = [
        pltpu.VMEM((first.shape[0] // parts, first.shape[1]), first.dtype)
        for (first, _), parts in zip(pairs, cuts)
        for _ in range(parts)
    ]
    return pl.pallas_call(
        functools.partial(choose_kernel, cuts),
        out_shape=shapes,
        in_specs=[SMEM] + [ANY] * (2 * len(pairs) + 1),
        out_specs=[VMEM] * len(shapes),
        scratch_shapes=[pltpu.SemaphoreType.DMA((len(shapes),))],
        compiler_params=limit(8),
        name="choose",
    )(where, *(piece for pair in pairs for piece in pair), after)


def cut_kernel(piece, *refs):
    out_refs, sems = refs[:-1], refs[-1]
    size = out_refs[0].shape[0]
    copies = [pltpu.make_async_copy(piece.at[pl.ds(n * size, size)], out, sems.at[n]) for n, out in enumerate(out_refs)]
    for copy in copies:
        copy.start()
    for copy in copies:
        copy.wait()


def cut(piece):
    part = pltpu.VMEM((piece.shape[0] // PARTS, piece.shape[1]), piece.dtype)
    return pl.pallas_call(
        cut_kernel,
        out_shape=[part] * PARTS,
        in_specs=[ANY],
        out_specs=[VMEM] * PARTS,
        scratch_shapes=[pltpu.SemaphoreType.DMA((PARTS,))],
        compiler_params=limit(2),
        name="cut",
    )(piece)


def tie_kernel(*refs):
    pass


def tied(array, after):
    return pl.pallas_call(
        tie_kernel,
        out_shape=jax.ShapeDtypeStruct(array.shape, array.dtype),
        in_specs=[ANY] * 2,
        out_specs=ANY,
        input_output_aliases={0: 0},
        compiler_params=limit(1),
        name="tied",
    )(array, after)


class Bringer:
    def __init__(self, a_ref, b_ref, sems, row_count, col_count):
        self.refs = {"a": (a_ref, a_ref.shape[0] // row_count), "b": (b_ref, b_ref.shape[0] // col_count)}
        self.sems, self.copies = sems, []

    def bring(self, which, ref, member, part=0, parts=1):
        target, size = self.refs[which]
        size //= parts
        rows = target.at[pl.ds(pl.multiple_of((member * parts + part) * size, size), size)]
        self.copies.append(pltpu.make_async_copy(ref, rows, self.sems.at[len(self.copies)]))
        self.copies[-1].start()

    def wait(self):
        for copy in self.copies:
            copy.wait()


def bring_chip(bringer, refs, shift, j, chips, parts=1):
    z, core = j // CORES, j % CORES
    for ref_core in (core, CORES - 1 - core):
        for part in range(parts):
            bringer.bring("b", refs.pop(0), (z - shift + chips) % chips * CORES + ref_core, part, parts)


def bring_first(bringer, refs, i, j, row_count, col_count):
    refs = list(refs)
    y_count, chips = row_count // SIDE, col_count // CORES
    y, x = i // SIDE, i % SIDE
    bringer.bring("a", refs.pop(0), i)
    bringer.bring("a", refs.pop(0), y * SIDE + SIDE - 1 - x)
    for shift in range(1, y_count):
        bringer.bring("a", refs.pop(0), (y - shift + y_count) % y_count * SIDE + x)
    for shift in (0, 1, chips - 1):
        bring_chip(bringer, refs, shift, j, chips)


def bring_rest(bringer, refs, i, j, row_count, col_count):
    refs = list(refs)
    y_count, chips = row_count // SIDE, col_count // CORES
    y, x = i // SIDE, i % SIDE
    for shift in range(1, y_count):
        bringer.bring("a", refs.pop(0), (y - shift + y_count) % y_count * SIDE + SIDE - 1 - x)
    for shift in range(2, chips // 2):
        bring_chip(bringer, refs, shift, j, chips)
        bring_chip(bringer, refs, chips - shift, j, chips)
    bring_chip(bringer, refs, chips // 2, j, chips, PARTS)


class Layout:
    def __init__(self, row_count, col_count, b_slots, kept_count):
        self.count = 2 * col_count * b_slots + UNROLL
        self.i, self.j = self.count + 1, self.count + 2
        self.pos = self.count + 3
        self.source = self.pos + kept_count
        self.size = self.source + SCAP * row_count * col_count + 1


def multiply_listed(listed, count, a_ref, b_ref, total):
    block = a_ref.shape[-1]

    def block_of(ref, index):
        return ref[pl.ds(pl.multiple_of(index * block, block), block), :]

    def multiply(step, carry):
        entries = [listed[step * UNROLL + u] for u in range(UNROLL)]
        products = [
            jnp.dot(
                block_of(a_ref, (entry >> 10) & 1023),
                block_of(b_ref, entry & 1023),
                preferred_element_type=jnp.float32,
            )
            for entry in entries
        ]
        for entry, product in zip(entries, products):
            q = entry >> 20
            total[q] = total[q] + product
        return carry

    lax.fori_loop(0, (count + UNROLL - 1) // UNROLL, multiply, 0)


def first_kernel(sizes, parts, keep, pos, where, exchange, *refs):
    row_count, col_count, b_slots = sizes
    pieces, refs = refs[:parts], refs[parts:]
    a_ref, b_ref, total, plan, ids, places, table, slot_rows, slot_table, listed, sems, sem = refs
    i, j = where[0], where[1]
    kept_count = keep.shape[0]
    panel_width = RB * col_count // row_count
    chips = col_count // CORES
    capacity = SCAP * row_count * col_count
    layout = Layout(row_count, col_count, b_slots, kept_count)
    bringer = Bringer(a_ref, b_ref, sems, row_count, col_count)
    bring_first(bringer, pieces, i, j, row_count, col_count)

    slot_rows[...] = exchange[:, 0, :]
    to_slot_table = pltpu.make_async_copy(slot_rows, slot_table, sem.at[0])
    to_slot_table.start()

    halves = col_count // row_count
    for half_panel in range(col_count):
        member, half = half_panel // halves, half_panel % halves
        rows = exchange[member * col_count + j, pl.ds(1, 1), :]
        ids[pl.ds(half_panel, 1), :] = rows if half == 0 else pltpu.roll(rows, LANES - half * b_slots, 1)
        source = half * row_count + (member + j - i + row_count) % row_count
        ids[pl.ds(col_count + half_panel, 1), :] = exchange[i * col_count + source, pl.ds(2, 1), :]
    rows = ids[pl.ds(0, col_count), :] * panel_width
    cols = ids[pl.ds(col_count, col_count), :]
    even = lax.broadcasted_iota(jnp.int32, cols.shape, 1) % 2 == 0
    crossed = jnp.where(even, pltpu.roll(cols, LANES - 1, 1), pltpu.roll(cols, 1, 1))
    for cross, columns in enumerate([cols, crossed]):
        target = rows + columns
        found = jnp.full_like(target, kept_count)
        for q in range(kept_count):
            found = jnp.where(target == keep[q], q, found)
        places[pl.ds(cross * col_count, col_count), :] = found
    to_table = pltpu.make_async_copy(places, table, sem.at[1])
    to_table.start()
    total[...] = jnp.zeros_like(total)
    to_table.wait()

    def look(half_panel, counts):
        member = half_panel // halves
        source = (half_panel % halves) * row_count + (member + j - i + row_count) % row_count
        a_near = (member % SIDE == i % SIDE) | (member // SIDE == i // SIDE)
        apart = jnp.abs(j // CORES - source // CORES)
        b_near = (apart <= 1) | (apart == chips - 1)

        def scan(into, n):
            for slot in range(b_slots):
                for cross in range(2):
                    q = table[cross * col_count + half_panel, slot]
                    into[n] = (q << 20) | ((half_panel * b_slots + slot) << 10) | (source * b_slots + (slot ^ cross))
                    n = n + (q < kept_count).astype(jnp.int32)
            return n

        return lax.cond(
            a_near & b_near,
            lambda near, far: (scan(listed, near), far),
            lambda near, far: (near, scan(plan, far)),
            *counts,
        )

    near, far = lax.fori_loop(0, col_count, look, (jnp.int32(0), jnp.int32(0)))
    for extra in range(UNROLL):
        listed[near + extra] = kept_count << 20
        plan[far + extra] = kept_count << 20
    plan[layout.count], plan[layout.i], plan[layout.j] = far, i, j
    for q in range(kept_count):
        plan[layout.pos + q] = pos[q]

    def clear(s, carry):
        plan[layout.source + s] = -1
        return carry

    lax.fori_loop(0, capacity + 1, clear, 0, unroll=5)
    to_slot_table.wait()

    def mark(d, carry):
        for m in range(SCAP):
            plan[layout.source + slot_table[d, m]] = by_column(d, row_count, col_count) * SCAP + m
        return carry

    lax.fori_loop(0, row_count * col_count, mark, 0, unroll=8)
    bringer.wait()
    multiply_listed(listed, near, a_ref, b_ref, total)


def first_products(sizes, keep, pos, where, exchange, pieces):
    row_count, col_count, b_slots = sizes
    block, kept_count = pieces[0].shape[-1], keep.shape[0]
    rows = col_count * b_slots * block
    return pl.pallas_call(
        functools.partial(first_kernel, sizes, len(pieces)),
        out_shape=[
            pltpu.VMEM((rows, block), jnp.bfloat16),
            pltpu.VMEM((rows, block), jnp.bfloat16),
            pltpu.VMEM((kept_count + 1, block, block), jnp.float32),
            jax.ShapeDtypeStruct((Layout(row_count, col_count, b_slots, kept_count).size,), jnp.int32),
        ],
        in_specs=[SMEM] * 3 + [VMEM] + [ANY] * len(pieces),
        out_specs=[VMEM] * 3 + [SMEM],
        scratch_shapes=[
            pltpu.VMEM((2 * col_count, LANES), jnp.int32),
            pltpu.VMEM((2 * col_count, LANES), jnp.int32),
            pltpu.SMEM((2 * col_count, LANES), jnp.int32),
            pltpu.VMEM((row_count * col_count, LANES), jnp.int32),
            pltpu.SMEM((row_count * col_count, LANES), jnp.int32),
            pltpu.SMEM((2 * col_count * b_slots + UNROLL,), jnp.int32),
            pltpu.SemaphoreType.DMA((len(pieces),)),
            pltpu.SemaphoreType.DMA((2,)),
        ],
        compiler_params=limit(26),
        cost_estimate=pl.CostEstimate(flops=1, bytes_accessed=0, transcendentals=0),
        name="first_products",
    )(keep, pos, where, exchange, *pieces)


def rest_kernel(sizes, parts, plan, *refs):
    row_count, col_count, b_slots = sizes
    pieces, refs = refs[3:3 + parts], refs[3 + parts:]
    a_ref, b_ref, total, send_ref, kept, sems, sem = refs
    kept_count = kept.shape[0]
    layout = Layout(row_count, col_count, b_slots, kept_count)
    bringer = Bringer(a_ref, b_ref, sems, row_count, col_count)
    bring_rest(bringer, pieces, plan[layout.i], plan[layout.j], row_count, col_count)
    bringer.wait()
    multiply_listed(plan, plan[layout.count], a_ref, b_ref, total)

    def finish(q, carry):
        kept[q] = total[q].astype(jnp.bfloat16)
        pltpu.make_async_copy(kept.at[q], send_ref.at[plan[layout.pos + q]], sem).start()
        return carry

    lax.fori_loop(0, kept_count, finish, 0, unroll=2)
    pltpu.make_async_copy(kept, kept, sem).wait()


def rest_products(sizes, kept_count, plan, buffers, pieces):
    row_count, col_count = sizes[:2]
    block = pieces[0].shape[-1]
    return pl.pallas_call(
        functools.partial(rest_kernel, sizes, len(pieces)),
        out_shape=[pltpu.VMEM(b.shape, b.dtype) for b in buffers]
        + [pltpu.HBM((SCAP * row_count * col_count, block, block), jnp.bfloat16)],
        in_specs=[SMEM] + [VMEM] * 3 + [ANY] * len(pieces),
        out_specs=[VMEM] * 3 + [HBM],
        scratch_shapes=[
            pltpu.VMEM((kept_count, block, block), jnp.bfloat16),
            pltpu.SemaphoreType.DMA((len(pieces),)),
            pltpu.SemaphoreType.DMA,
        ],
        input_output_aliases={1 + n: n for n in range(3)},
        compiler_params=limit(28),
        name="rest_products",
    )(plan, *buffers, *pieces)[-1]


def place_kernel(layout, plan, recv_ref, out_ref, zero, sem):
    zero[...] = jnp.zeros_like(zero)

    def place(s, carry):
        r = plan[layout.source + s]

        @pl.when(r >= 0)
        def _():
            pltpu.make_async_copy(recv_ref.at[r], out_ref.at[s], sem).start()

        @pl.when(r < 0)
        def _():
            pltpu.make_async_copy(zero, out_ref.at[s], sem).start()

        return carry

    lax.fori_loop(0, out_ref.shape[0], place, 0, unroll=4)
    pltpu.make_async_copy(recv_ref, out_ref, sem).wait()


def place(layout, plan, recv):
    block = recv.shape[-1]
    return pl.pallas_call(
        functools.partial(place_kernel, layout),
        out_shape=jax.ShapeDtypeStruct(recv.shape, recv.dtype),
        in_specs=[SMEM, VMEM],
        out_specs=HBM,
        scratch_shapes=[pltpu.VMEM((block, block), jnp.bfloat16), pltpu.SemaphoreType.DMA],
        compiler_params=limit(12),
        name="place",
    )(plan, recv)


def gathered(a_own, b_own, row_count, col_count, where, outgoing, multiply_near):
    chips, shifts = col_count // CORES, range(1, row_count // SIDE)

    def moved(piece, target):
        pairs = [(d, c, target(d, c)) for d in range(row_count) for c in range(col_count)]
        return lax.ppermute(
            piece, ("row", "col"), [(d * col_count + c, to[0] * col_count + to[1]) for d, c, to in pairs]
        )

    def around(d, c, by, other=False):
        core = CORES - 1 - c % CORES if other else c % CORES
        return d, (c // CORES + by) % chips * CORES + core

    def along(d, c, shift):
        return (d + shift * SIDE) % row_count, c

    def swapped(piece):
        return moved(piece, lambda d, c: around(d, c, 0, True))

    below = [moved(b_own, lambda d, c: around(d, c, 1))]
    above = [moved(b_own, lambda d, c: around(d, c, -1))]
    beside = moved(a_own, lambda d, c: (d ^ 1, c))
    ahead = [moved(a_own, lambda d, c, shift=shift: along(d, c, shift)) for shift in shifts]
    exchange = lax.all_to_all(outgoing, ("row", "col"), split_axis=0, concat_axis=0, tiled=True)
    for _ in range(2, chips // 2):
        below.append(moved(below[-1], lambda d, c: around(d, c, 1)))
        above.append(moved(above[-1], lambda d, c: around(d, c, -1)))
    crossing = choose(where, [(piece, beside) for piece in ahead], [1] * len(ahead), exchange)
    opposite = moved(above[-1], lambda d, c: around(d, c, -1))
    diagonal = [
        moved(piece, lambda d, c, shift=shift: (d ^ 1, c) if c % CORES == 0 else along(d, c, shift))
        for shift, piece in zip(shifts, crossing)
    ]

    near = [a_own, beside, *ahead]
    for piece in (b_own, below[0], above[0]):
        near += [piece, swapped(piece)]
    *buffers, plan = multiply_near(exchange, near)
    opposite = list(cut(tied(opposite, plan)))
    crossed = [swapped(opposite[0])]
    opposite[1] = tied(opposite[1], crossed[0])
    crossed.append(swapped(opposite[1]))
    far = list(diagonal)
    for n in range(1, chips // 2 - 1):
        far += [below[n], swapped(below[n]), above[n], swapped(above[n])]
    return buffers, plan, far + opposite + crossed


def body(a_blocks, a_rows, b_blocks, b_cols, c_keep, c_owner, c_slot):
    row_count = lax.axis_size("row")
    col_count = lax.axis_size("col")
    block = a_blocks.shape[-1]
    keep, owner_ids, slot_ids = c_keep[0, 0], c_owner[0, 0], c_slot[0, 0]
    sizes = (row_count, col_count, b_cols.shape[1])
    where = jnp.stack([lax.axis_index("row"), lax.axis_index("col")]).astype(jnp.int32)

    outgoing, pos = announce(row_count, col_count, owner_ids, slot_ids, a_rows, b_cols)

    buffers, plan, far = gathered(
        a_blocks[0].reshape(-1, block),
        b_blocks[0].reshape(-1, block),
        row_count,
        col_count,
        where,
        outgoing,
        functools.partial(first_products, sizes, keep, pos, where),
    )
    send = rest_products(sizes, keep.shape[0], plan, buffers, far)
    recv = lax.all_to_all(send, ("col", "row"), split_axis=0, concat_axis=0, tiled=True)
    return place(Layout(*sizes, keep.shape[0]), plan, recv)[None]


def solution(mesh):
    return jax.shard_map(
        body,
        mesh=mesh,
        in_specs=(
            P("col", "row", None, None),
            P("col", "row"),
            P("row", "col", None, None),
            P("row", "col"),
            P("row", "col", None),
            P("row", "col", None),
            P("row", "col", None),
        ),
        out_specs=P("row", "col", None, None),
        check_vma=False,
    )
```

```python
import functools

import jax
import jax.numpy as jnp
from jax import lax
from jax.experimental import pallas as pl
from jax.experimental.pallas import tpu as pltpu
from jax.sharding import PartitionSpec as P

RB = 8
SCAP = 2
UNROLL = 8
CORES = 2
SIDE = 2
PARTS = 2
EXCHANGE_ROWS = 8
LANES = 128

SMEM = pl.BlockSpec(memory_space=pltpu.SMEM)
VMEM = pl.BlockSpec(memory_space=pltpu.VMEM)
HBM = pl.BlockSpec(memory_space=pltpu.HBM)
ANY = pl.BlockSpec(memory_space=pl.ANY)


def limit(megabytes):
    return pltpu.CompilerParams(vmem_limit_bytes=megabytes * 1024 * 1024)


def by_column(device, row_count, col_count):
    return device % col_count * row_count + device // col_count


def announce_kernel(row_count, col_count, told, ids, out_ref, pos, base, sent):
    kept_count = pos.shape[0]
    base[...] = jnp.zeros_like(base)
    base[pl.ds(0, 1), :] = jnp.full((1, LANES), SCAP * out_ref.shape[0], jnp.int32)
    base[pl.ds(1, 1), pl.ds(0, ids.shape[1])] = ids[...]
    out_ref[...] = jnp.broadcast_to(base[...][None], out_ref.shape)
    lane = lax.broadcasted_iota(jnp.int32, (1, LANES), 1)

    def clear(d, carry):
        sent[d] = 0
        return carry

    lax.fori_loop(0, out_ref.shape[0], clear, 0, unroll=8)

    def tell(q, carry):
        owner = told[q]
        order = sent[owner]
        pos[q] = by_column(owner, row_count, col_count) * SCAP + order
        sent[owner] = order + 1
        place = by_column(owner, row_count, col_count)
        out_ref[place, pl.ds(0, 1), :] = jnp.where(lane == order, told[kept_count + q], out_ref[place, pl.ds(0, 1), :])
        return carry

    lax.fori_loop(0, kept_count, tell, 0)


def announce(row_count, col_count, owners, slots, a_ids, b_ids):
    return pl.pallas_call(
        functools.partial(announce_kernel, row_count, col_count),
        out_shape=[
            pltpu.VMEM((row_count * col_count, EXCHANGE_ROWS, LANES), jnp.int32),
            jax.ShapeDtypeStruct(owners.shape, jnp.int32),
        ],
        in_specs=[SMEM, VMEM],
        out_specs=[VMEM, SMEM],
        scratch_shapes=[pltpu.VMEM((EXCHANGE_ROWS, LANES), jnp.int32), pltpu.SMEM((row_count * col_count,), jnp.int32)],
        compiler_params=limit(2),
        name="announce",
    )(jnp.concatenate([owners, slots]), jnp.concatenate([a_ids, b_ids], axis=1))


def choose_kernel(cuts, where, *refs):
    count = len(cuts)
    pairs = [(refs[2 * n], refs[2 * n + 1]) for n in range(count)]
    out_refs, sems = list(refs[2 * count + 1:-1]), refs[-1]
    core = where[1] % CORES
    waits = []
    for (first, second), parts in zip(pairs, cuts):
        size = first.shape[0] // parts
        for part in range(parts):
            out, sem, rows = out_refs[len(waits)], sems.at[len(waits)], pl.ds(part * size, size)
            pl.when(core == 0)(pltpu.make_async_copy(first.at[rows], out, sem).start)
            pl.when(core != 0)(pltpu.make_async_copy(second.at[rows], out, sem).start)
            waits.append(pltpu.make_async_copy(first.at[rows], out, sem))
    for copy in waits:
        copy.wait()


def choose(where, pairs, cuts, after):
    shapes = [
        pltpu.VMEM((first.shape[0] // parts, first.shape[1]), first.dtype)
        for (first, _), parts in zip(pairs, cuts)
        for _ in range(parts)
    ]
    return pl.pallas_call(
        functools.partial(choose_kernel, cuts),
        out_shape=shapes,
        in_specs=[SMEM] + [ANY] * (2 * len(pairs) + 1),
        out_specs=[VMEM] * len(shapes),
        scratch_shapes=[pltpu.SemaphoreType.DMA((len(shapes),))],
        compiler_params=limit(8),
        name="choose",
    )(where, *(piece for pair in pairs for piece in pair), after)


def cut_kernel(piece, *refs):
    out_refs, sems = refs[:-1], refs[-1]
    size = out_refs[0].shape[0]
    copies = [pltpu.make_async_copy(piece.at[pl.ds(n * size, size)], out, sems.at[n]) for n, out in enumerate(out_refs)]
    for copy in copies:
        copy.start()
    for copy in copies:
        copy.wait()


def cut(piece):
    part = pltpu.VMEM((piece.shape[0] // PARTS, piece.shape[1]), piece.dtype)
    return pl.pallas_call(
        cut_kernel,
        out_shape=[part] * PARTS,
        in_specs=[ANY],
        out_specs=[VMEM] * PARTS,
        scratch_shapes=[pltpu.SemaphoreType.DMA((PARTS,))],
        compiler_params=limit(2),
        name="cut",
    )(piece)


def tie_kernel(*refs):
    pass


def tied(array, after):
    return pl.pallas_call(
        tie_kernel,
        out_shape=jax.ShapeDtypeStruct(array.shape, array.dtype),
        in_specs=[ANY] * 2,
        out_specs=ANY,
        input_output_aliases={0: 0},
        compiler_params=limit(1),
        name="tied",
    )(array, after)


class Bringer:
    def __init__(self, a_ref, b_ref, sems, row_count, col_count):
        self.refs = {"a": (a_ref, a_ref.shape[0] // row_count), "b": (b_ref, b_ref.shape[0] // col_count)}
        self.sems, self.copies = sems, []

    def bring(self, which, ref, member, part=0, parts=1):
        target, size = self.refs[which]
        size //= parts
        rows = target.at[pl.ds(pl.multiple_of((member * parts + part) * size, size), size)]
        self.copies.append(pltpu.make_async_copy(ref, rows, self.sems.at[len(self.copies)]))
        self.copies[-1].start()

    def wait(self):
        for copy in self.copies:
            copy.wait()


def bring_chip(bringer, refs, shift, j, chips, parts=1):
    z, core = j // CORES, j % CORES
    for ref_core in (core, CORES - 1 - core):
        for part in range(parts):
            bringer.bring("b", refs.pop(0), (z - shift + chips) % chips * CORES + ref_core, part, parts)


def bring_first(bringer, refs, i, j, row_count, col_count):
    refs = list(refs)
    y_count, chips = row_count // SIDE, col_count // CORES
    y, x = i // SIDE, i % SIDE
    bringer.bring("a", refs.pop(0), i)
    bringer.bring("a", refs.pop(0), y * SIDE + SIDE - 1 - x)
    for shift in range(1, y_count):
        bringer.bring("a", refs.pop(0), (y - shift + y_count) % y_count * SIDE + x)
    for shift in (0, 1, chips - 1):
        bring_chip(bringer, refs, shift, j, chips)


def bring_rest(bringer, refs, i, j, row_count, col_count):
    refs = list(refs)
    y_count, chips = row_count // SIDE, col_count // CORES
    y, x = i // SIDE, i % SIDE
    for shift in range(1, y_count):
        bringer.bring("a", refs.pop(0), (y - shift + y_count) % y_count * SIDE + SIDE - 1 - x)
    for shift in range(2, chips // 2):
        bring_chip(bringer, refs, shift, j, chips)
        bring_chip(bringer, refs, chips - shift, j, chips)
    bring_chip(bringer, refs, chips // 2, j, chips, PARTS)


class Layout:
    def __init__(self, row_count, col_count, b_slots, kept_count):
        self.count = 2 * col_count * b_slots + UNROLL
        self.i, self.j = self.count + 1, self.count + 2
        self.pos = self.count + 3
        self.source = self.pos + kept_count
        self.size = self.source + SCAP * row_count * col_count + 1


def multiply_listed(listed, count, a_ref, b_ref, total):
    block = a_ref.shape[-1]

    def block_of(ref, index):
        return ref[pl.ds(pl.multiple_of(index * block, block), block), :]

    def multiply(step, carry):
        entries = [listed[step * UNROLL + u] for u in range(UNROLL)]
        products = [
            jnp.dot(
                block_of(a_ref, (entry >> 10) & 1023),
                block_of(b_ref, entry & 1023),
                preferred_element_type=jnp.float32,
            )
            for entry in entries
        ]
        for entry, product in zip(entries, products):
            q = entry >> 20
            total[q] = total[q] + product
        return carry

    lax.fori_loop(0, (count + UNROLL - 1) // UNROLL, multiply, 0)


def first_kernel(sizes, parts, keep, pos, where, exchange, *refs):
    row_count, col_count, b_slots = sizes
    pieces, refs = refs[:parts], refs[parts:]
    a_ref, b_ref, total, plan, ids, places, table, slot_rows, slot_table, listed, sems, sem = refs
    i, j = where[0], where[1]
    kept_count = keep.shape[0]
    panel_width = RB * col_count // row_count
    chips = col_count // CORES
    capacity = SCAP * row_count * col_count
    layout = Layout(row_count, col_count, b_slots, kept_count)
    bringer = Bringer(a_ref, b_ref, sems, row_count, col_count)
    bring_first(bringer, pieces, i, j, row_count, col_count)

    slot_rows[...] = exchange[:, 0, :]
    to_slot_table = pltpu.make_async_copy(slot_rows, slot_table, sem.at[0])
    to_slot_table.start()

    halves = col_count // row_count
    for half_panel in range(col_count):
        member, half = half_panel // halves, half_panel % halves
        rows = exchange[j * row_count + member, pl.ds(1, 1), :]
        ids[pl.ds(half_panel, 1), :] = rows if half == 0 else pltpu.roll(rows, LANES - half * b_slots, 1)
        source = half * row_count + (member + j - i + row_count) % row_count
        cols = exchange[source * row_count + i, pl.ds(1, 1), :]
        ids[pl.ds(col_count + half_panel, 1), :] = pltpu.roll(cols, LANES - halves * b_slots, 1)
    rows = ids[pl.ds(0, col_count), :] * panel_width
    cols = ids[pl.ds(col_count, col_count), :]
    even = lax.broadcasted_iota(jnp.int32, cols.shape, 1) % 2 == 0
    crossed = jnp.where(even, pltpu.roll(cols, LANES - 1, 1), pltpu.roll(cols, 1, 1))
    for cross, columns in enumerate([cols, crossed]):
        target = rows + columns
        found = jnp.full_like(target, kept_count)
        for q in range(kept_count):
            found = jnp.where(target == keep[q], q, found)
        places[pl.ds(cross * col_count, col_count), :] = found
    to_table = pltpu.make_async_copy(places, table, sem.at[1])
    to_table.start()
    total[...] = jnp.zeros_like(total)
    to_table.wait()

    def look(half_panel, counts):
        member = half_panel // halves
        source = (half_panel % halves) * row_count + (member + j - i + row_count) % row_count
        a_near = (member % SIDE == i % SIDE) | (member // SIDE == i // SIDE)
        apart = jnp.abs(j // CORES - source // CORES)
        b_near = (apart <= 1) | (apart == chips - 1)

        def scan(into, n):
            for slot in range(b_slots):
                for cross in range(2):
                    q = table[cross * col_count + half_panel, slot]
                    into[n] = (q << 20) | ((half_panel * b_slots + slot) << 10) | (source * b_slots + (slot ^ cross))
                    n = n + (q < kept_count).astype(jnp.int32)
            return n

        return lax.cond(
            a_near & b_near,
            lambda near, far: (scan(listed, near), far),
            lambda near, far: (near, scan(plan, far)),
            *counts,
        )

    near, far = lax.fori_loop(0, col_count, look, (jnp.int32(0), jnp.int32(0)))
    for extra in range(UNROLL):
        listed[near + extra] = kept_count << 20
        plan[far + extra] = kept_count << 20
    plan[layout.count], plan[layout.i], plan[layout.j] = far, i, j
    for q in range(kept_count):
        plan[layout.pos + q] = pos[q]

    def clear(s, carry):
        plan[layout.source + s] = -1
        return carry

    lax.fori_loop(0, capacity + 1, clear, 0, unroll=5)
    to_slot_table.wait()

    def mark(d, carry):
        for m in range(SCAP):
            plan[layout.source + slot_table[d, m]] = d * SCAP + m
        return carry

    lax.fori_loop(0, row_count * col_count, mark, 0, unroll=8)
    bringer.wait()
    multiply_listed(listed, near, a_ref, b_ref, total)


def first_products(sizes, keep, pos, where, exchange, pieces):
    row_count, col_count, b_slots = sizes
    block, kept_count = pieces[0].shape[-1], keep.shape[0]
    rows = col_count * b_slots * block
    return pl.pallas_call(
        functools.partial(first_kernel, sizes, len(pieces)),
        out_shape=[
            pltpu.VMEM((rows, block), jnp.bfloat16),
            pltpu.VMEM((rows, block), jnp.bfloat16),
            pltpu.VMEM((kept_count + 1, block, block), jnp.float32),
            jax.ShapeDtypeStruct((Layout(row_count, col_count, b_slots, kept_count).size,), jnp.int32),
        ],
        in_specs=[SMEM] * 3 + [VMEM] + [ANY] * len(pieces),
        out_specs=[VMEM] * 3 + [SMEM],
        scratch_shapes=[
            pltpu.VMEM((2 * col_count, LANES), jnp.int32),
            pltpu.VMEM((2 * col_count, LANES), jnp.int32),
            pltpu.SMEM((2 * col_count, LANES), jnp.int32),
            pltpu.VMEM((row_count * col_count, LANES), jnp.int32),
            pltpu.SMEM((row_count * col_count, LANES), jnp.int32),
            pltpu.SMEM((2 * col_count * b_slots + UNROLL,), jnp.int32),
            pltpu.SemaphoreType.DMA((len(pieces),)),
            pltpu.SemaphoreType.DMA((2,)),
        ],
        compiler_params=limit(26),
        cost_estimate=pl.CostEstimate(flops=1, bytes_accessed=0, transcendentals=0),
        name="first_products",
    )(keep, pos, where, exchange, *pieces)


def rest_kernel(sizes, parts, plan, *refs):
    row_count, col_count, b_slots = sizes
    pieces, refs = refs[3:3 + parts], refs[3 + parts:]
    a_ref, b_ref, total, send_ref, kept, sems, sem = refs
    kept_count = kept.shape[0]
    layout = Layout(row_count, col_count, b_slots, kept_count)
    bringer = Bringer(a_ref, b_ref, sems, row_count, col_count)
    bring_rest(bringer, pieces, plan[layout.i], plan[layout.j], row_count, col_count)
    bringer.wait()
    multiply_listed(plan, plan[layout.count], a_ref, b_ref, total)

    def finish(q, carry):
        kept[q] = total[q].astype(jnp.bfloat16)
        pltpu.make_async_copy(kept.at[q], send_ref.at[plan[layout.pos + q]], sem).start()
        return carry

    lax.fori_loop(0, kept_count, finish, 0, unroll=2)
    pltpu.make_async_copy(kept, kept, sem).wait()


def rest_products(sizes, kept_count, plan, buffers, pieces):
    row_count, col_count = sizes[:2]
    block = pieces[0].shape[-1]
    return pl.pallas_call(
        functools.partial(rest_kernel, sizes, len(pieces)),
        out_shape=[pltpu.VMEM(b.shape, b.dtype) for b in buffers]
        + [pltpu.HBM((SCAP * row_count * col_count, block, block), jnp.bfloat16)],
        in_specs=[SMEM] + [VMEM] * 3 + [ANY] * len(pieces),
        out_specs=[VMEM] * 3 + [HBM],
        scratch_shapes=[
            pltpu.VMEM((kept_count, block, block), jnp.bfloat16),
            pltpu.SemaphoreType.DMA((len(pieces),)),
            pltpu.SemaphoreType.DMA,
        ],
        input_output_aliases={1 + n: n for n in range(3)},
        compiler_params=limit(28),
        name="rest_products",
    )(plan, *buffers, *pieces)[-1]


def place_kernel(layout, plan, recv_ref, out_ref, zero, sem):
    zero[...] = jnp.zeros_like(zero)

    def place(s, carry):
        r = plan[layout.source + s]

        @pl.when(r >= 0)
        def _():
            pltpu.make_async_copy(recv_ref.at[r], out_ref.at[s], sem).start()

        @pl.when(r < 0)
        def _():
            pltpu.make_async_copy(zero, out_ref.at[s], sem).start()

        return carry

    lax.fori_loop(0, out_ref.shape[0], place, 0, unroll=4)
    pltpu.make_async_copy(recv_ref, out_ref, sem).wait()


def place(layout, plan, recv):
    block = recv.shape[-1]
    return pl.pallas_call(
        functools.partial(place_kernel, layout),
        out_shape=jax.ShapeDtypeStruct(recv.shape, recv.dtype),
        in_specs=[SMEM, VMEM],
        out_specs=HBM,
        scratch_shapes=[pltpu.VMEM((block, block), jnp.bfloat16), pltpu.SemaphoreType.DMA],
        compiler_params=limit(12),
        name="place",
    )(plan, recv)


def gathered(a_own, b_own, row_count, col_count, where, outgoing, multiply_near):
    chips, shifts = col_count // CORES, range(1, row_count // SIDE)

    def moved(piece, target):
        pairs = [(d, c, target(d, c)) for d in range(row_count) for c in range(col_count)]
        return lax.ppermute(
            piece, ("row", "col"), [(d * col_count + c, to[0] * col_count + to[1]) for d, c, to in pairs]
        )

    def around(d, c, by, other=False):
        core = CORES - 1 - c % CORES if other else c % CORES
        return d, (c // CORES + by) % chips * CORES + core

    def along(d, c, shift):
        return (d + shift * SIDE) % row_count, c

    def swapped(piece):
        return moved(piece, lambda d, c: around(d, c, 0, True))

    below = [moved(b_own, lambda d, c: around(d, c, 1))]
    above = [moved(b_own, lambda d, c: around(d, c, -1))]
    beside = moved(a_own, lambda d, c: (d ^ 1, c))
    ahead = [moved(a_own, lambda d, c, shift=shift: along(d, c, shift)) for shift in shifts]
    exchange = lax.all_to_all(outgoing, ("col", "row"), split_axis=0, concat_axis=0, tiled=True)
    for _ in range(2, chips // 2):
        below.append(moved(below[-1], lambda d, c: around(d, c, 1)))
        above.append(moved(above[-1], lambda d, c: around(d, c, -1)))
    crossing = choose(where, [(piece, beside) for piece in ahead], [1] * len(ahead), exchange)
    opposite = moved(above[-1], lambda d, c: around(d, c, -1))
    diagonal = [
        moved(piece, lambda d, c, shift=shift: (d ^ 1, c) if c % CORES == 0 else along(d, c, shift))
        for shift, piece in zip(shifts, crossing)
    ]

    near = [a_own, beside, *ahead]
    for piece in (b_own, below[0], above[0]):
        near += [piece, swapped(piece)]
    *buffers, plan = multiply_near(exchange, near)
    opposite = list(cut(tied(opposite, plan)))
    crossed = [swapped(opposite[0])]
    opposite[1] = tied(opposite[1], crossed[0])
    crossed.append(swapped(opposite[1]))
    far = list(diagonal)
    for n in range(1, chips // 2 - 1):
        far += [below[n], swapped(below[n]), above[n], swapped(above[n])]
    return buffers, plan, far + opposite + crossed


def body(a_blocks, a_rows, b_blocks, b_cols, c_keep, c_owner, c_slot):
    row_count = lax.axis_size("row")
    col_count = lax.axis_size("col")
    block = a_blocks.shape[-1]
    keep, owner_ids, slot_ids = c_keep[0, 0], c_owner[0, 0], c_slot[0, 0]
    sizes = (row_count, col_count, b_cols.shape[1])
    where = jnp.stack([lax.axis_index("row"), lax.axis_index("col")]).astype(jnp.int32)

    outgoing, pos = announce(row_count, col_count, owner_ids, slot_ids, a_rows, b_cols)

    buffers, plan, far = gathered(
        a_blocks[0].reshape(-1, block),
        b_blocks[0].reshape(-1, block),
        row_count,
        col_count,
        where,
        outgoing,
        functools.partial(first_products, sizes, keep, pos, where),
    )
    send = rest_products(sizes, keep.shape[0], plan, buffers, far)
    recv = lax.all_to_all(send, ("col", "row"), split_axis=0, concat_axis=0, tiled=True)
    return place(Layout(*sizes, keep.shape[0]), plan, recv)[None]


def solution(mesh):
    return jax.shard_map(
        body,
        mesh=mesh,
        in_specs=(
            P("col", "row", None, None),
            P("col", "row"),
            P("row", "col", None, None),
            P("row", "col"),
            P("row", "col", None),
            P("row", "col", None),
            P("row", "col", None),
        ),
        out_specs=P("row", "col", None, None),
        check_vma=False,
    )
```

```python
import functools

import jax
import jax.numpy as jnp
from jax import lax
from jax.experimental import pallas as pl
from jax.experimental.pallas import tpu as pltpu
from jax.sharding import PartitionSpec as P

RB = 8
SCAP = 2
UNROLL = 8
CORES = 2
SIDE = 2
PARTS = 2
EXCHANGE_ROWS = 8
LANES = 128

SMEM = pl.BlockSpec(memory_space=pltpu.SMEM)
VMEM = pl.BlockSpec(memory_space=pltpu.VMEM)
HBM = pl.BlockSpec(memory_space=pltpu.HBM)
ANY = pl.BlockSpec(memory_space=pl.ANY)


def limit(megabytes):
    return pltpu.CompilerParams(vmem_limit_bytes=megabytes * 1024 * 1024)


def by_column(device, row_count, col_count):
    return device % col_count * row_count + device // col_count


def announce_kernel(row_count, col_count, told, ids, piece, out_ref, copy_ref, pos, base, sent, sem):
    copy = pltpu.make_async_copy(piece, copy_ref, sem)
    copy.start()
    kept_count = pos.shape[0]
    base[...] = jnp.zeros_like(base)
    base[pl.ds(0, 1), :] = jnp.full((1, LANES), SCAP * out_ref.shape[0], jnp.int32)
    base[pl.ds(1, 1), pl.ds(0, ids.shape[1])] = ids[...]
    out_ref[...] = jnp.broadcast_to(base[...][None], out_ref.shape)
    lane = lax.broadcasted_iota(jnp.int32, (1, LANES), 1)

    def clear(d, carry):
        sent[d] = 0
        return carry

    lax.fori_loop(0, out_ref.shape[0], clear, 0, unroll=8)

    def tell(q, carry):
        owner = told[q]
        order = sent[owner]
        pos[q] = by_column(owner, row_count, col_count) * SCAP + order
        sent[owner] = order + 1
        place = by_column(owner, row_count, col_count)
        out_ref[place, pl.ds(0, 1), :] = jnp.where(lane == order, told[kept_count + q], out_ref[place, pl.ds(0, 1), :])
        return carry

    lax.fori_loop(0, kept_count, tell, 0)
    copy.wait()


def announce(row_count, col_count, owners, slots, a_ids, b_ids, piece):
    return pl.pallas_call(
        functools.partial(announce_kernel, row_count, col_count),
        out_shape=[
            pltpu.VMEM((row_count * col_count, EXCHANGE_ROWS, LANES), jnp.int32),
            pltpu.VMEM(piece.shape, piece.dtype),
            jax.ShapeDtypeStruct(owners.shape, jnp.int32),
        ],
        in_specs=[SMEM, VMEM, ANY],
        out_specs=[VMEM, VMEM, SMEM],
        scratch_shapes=[pltpu.VMEM((EXCHANGE_ROWS, LANES), jnp.int32), pltpu.SMEM((row_count * col_count,), jnp.int32), pltpu.SemaphoreType.DMA],
        compiler_params=limit(2),
        name="announce",
    )(jnp.concatenate([owners, slots]), jnp.concatenate([a_ids, b_ids], axis=1), piece)


def choose_kernel(cuts, where, *refs):
    count = len(cuts)
    pairs = [(refs[2 * n], refs[2 * n + 1]) for n in range(count)]
    out_refs, sems = list(refs[2 * count + 1:-1]), refs[-1]
    core = where[1] % CORES
    waits = []
    for (first, second), parts in zip(pairs, cuts):
        size = first.shape[0] // parts
        for part in range(parts):
            out, sem, rows = out_refs[len(waits)], sems.at[len(waits)], pl.ds(part * size, size)
            pl.when(core == 0)(pltpu.make_async_copy(first.at[rows], out, sem).start)
            pl.when(core != 0)(pltpu.make_async_copy(second.at[rows], out, sem).start)
            waits.append(pltpu.make_async_copy(first.at[rows], out, sem))
    for copy in waits:
        copy.wait()


def choose(where, pairs, cuts, after):
    shapes = [
        pltpu.VMEM((first.shape[0] // parts, first.shape[1]), first.dtype)
        for (first, _), parts in zip(pairs, cuts)
        for _ in range(parts)
    ]
    return pl.pallas_call(
        functools.partial(choose_kernel, cuts),
        out_shape=shapes,
        in_specs=[SMEM] + [ANY] * (2 * len(pairs) + 1),
        out_specs=[VMEM] * len(shapes),
        scratch_shapes=[pltpu.SemaphoreType.DMA((len(shapes),))],
        compiler_params=limit(8),
        name="choose",
    )(where, *(piece for pair in pairs for piece in pair), after)


def cut_kernel(piece, *refs):
    out_refs, sems = refs[:-1], refs[-1]
    size = out_refs[0].shape[0]
    copies = [pltpu.make_async_copy(piece.at[pl.ds(n * size, size)], out, sems.at[n]) for n, out in enumerate(out_refs)]
    for copy in copies:
        copy.start()
    for copy in copies:
        copy.wait()


def cut(piece):
    part = pltpu.VMEM((piece.shape[0] // PARTS, piece.shape[1]), piece.dtype)
    return pl.pallas_call(
        cut_kernel,
        out_shape=[part] * PARTS,
        in_specs=[ANY],
        out_specs=[VMEM] * PARTS,
        scratch_shapes=[pltpu.SemaphoreType.DMA((PARTS,))],
        compiler_params=limit(2),
        name="cut",
    )(piece)


def tie_kernel(*refs):
    pass


def tied(array, *after):
    return pl.pallas_call(
        tie_kernel,
        out_shape=jax.ShapeDtypeStruct(array.shape, array.dtype),
        in_specs=[ANY] * (1 + len(after)),
        out_specs=ANY,
        input_output_aliases={0: 0},
        compiler_params=limit(1),
        name="tied",
    )(array, *after)


class Bringer:
    def __init__(self, a_ref, b_ref, sems, row_count, col_count):
        self.refs = {"a": (a_ref, a_ref.shape[0] // row_count), "b": (b_ref, b_ref.shape[0] // col_count)}
        self.sems, self.copies = sems, []

    def bring(self, which, ref, member, part=0, parts=1):
        target, size = self.refs[which]
        size //= parts
        rows = target.at[pl.ds(pl.multiple_of((member * parts + part) * size, size), size)]
        self.copies.append(pltpu.make_async_copy(ref, rows, self.sems.at[len(self.copies)]))
        self.copies[-1].start()

    def wait(self):
        for copy in self.copies:
            copy.wait()


def bring_chip(bringer, refs, shift, j, chips, parts=1):
    z, core = j // CORES, j % CORES
    for ref_core in (core, CORES - 1 - core):
        for part in range(parts):
            bringer.bring("b", refs.pop(0), (z - shift + chips) % chips * CORES + ref_core, part, parts)


def bring_first(bringer, refs, i, j, row_count, col_count):
    refs = list(refs)
    y_count, chips = row_count // SIDE, col_count // CORES
    y, x = i // SIDE, i % SIDE
    bringer.bring("a", refs.pop(0), i)
    bringer.bring("a", refs.pop(0), y * SIDE + SIDE - 1 - x)
    for shift in range(1, y_count):
        bringer.bring("a", refs.pop(0), (y - shift + y_count) % y_count * SIDE + x)
    for shift in (0, chips - 1):
        bring_chip(bringer, refs, shift, j, chips)
    z, core = j // CORES, j % CORES
    bringer.bring("b", refs.pop(0), (z - 1 + chips) % chips * CORES + core)


def bring_rest(bringer, refs, i, j, row_count, col_count):
    refs = list(refs)
    y_count, chips = row_count // SIDE, col_count // CORES
    y, x = i // SIDE, i % SIDE
    for shift in range(1, y_count):
        bringer.bring("a", refs.pop(0), (y - shift + y_count) % y_count * SIDE + SIDE - 1 - x)
    for shift in range(2, chips // 2):
        bring_chip(bringer, refs, shift, j, chips)
        bring_chip(bringer, refs, chips - shift, j, chips)
    z, core = j // CORES, j % CORES
    bringer.bring("b", refs.pop(0), (z - 1 + chips) % chips * CORES + CORES - 1 - core)
    bring_chip(bringer, refs, chips // 2, j, chips, PARTS)


class Layout:
    def __init__(self, row_count, col_count, b_slots, kept_count):
        self.count = 2 * col_count * b_slots + UNROLL
        self.i, self.j = self.count + 1, self.count + 2
        self.pos = self.count + 3
        self.source = self.pos + kept_count
        self.size = self.source + SCAP * row_count * col_count + 1


def multiply_listed(listed, count, a_ref, b_ref, total):
    block = a_ref.shape[-1]

    def block_of(ref, index):
        return ref[pl.ds(pl.multiple_of(index * block, block), block), :]

    def multiply(step, carry):
        entries = [listed[step * UNROLL + u] for u in range(UNROLL)]
        products = [
            jnp.dot(
                block_of(a_ref, (entry >> 10) & 1023),
                block_of(b_ref, entry & 1023),
                preferred_element_type=jnp.float32,
            )
            for entry in entries
        ]
        for entry, product in zip(entries, products):
            q = entry >> 20
            total[q] = total[q] + product
        return carry

    lax.fori_loop(0, (count + UNROLL - 1) // UNROLL, multiply, 0)


def first_kernel(sizes, parts, keep, pos, where, exchange, *refs):
    row_count, col_count, b_slots = sizes
    pieces, refs = refs[:parts], refs[parts:]
    a_ref, b_ref, total, plan, ids, places, table, slot_rows, slot_table, listed, sems, sem = refs
    i, j = where[0], where[1]
    kept_count = keep.shape[0]
    panel_width = RB * col_count // row_count
    chips = col_count // CORES
    capacity = SCAP * row_count * col_count
    layout = Layout(row_count, col_count, b_slots, kept_count)
    bringer = Bringer(a_ref, b_ref, sems, row_count, col_count)
    bring_first(bringer, pieces, i, j, row_count, col_count)

    slot_rows[...] = exchange[:, 0, :]
    to_slot_table = pltpu.make_async_copy(slot_rows, slot_table, sem.at[0])
    to_slot_table.start()

    halves = col_count // row_count
    for half_panel in range(col_count):
        member, half = half_panel // halves, half_panel % halves
        rows = exchange[j * row_count + member, pl.ds(1, 1), :]
        ids[pl.ds(half_panel, 1), :] = rows if half == 0 else pltpu.roll(rows, LANES - half * b_slots, 1)
        source = half * row_count + (member + j - i + row_count) % row_count
        cols = exchange[source * row_count + i, pl.ds(1, 1), :]
        ids[pl.ds(col_count + half_panel, 1), :] = pltpu.roll(cols, LANES - halves * b_slots, 1)
    rows = ids[pl.ds(0, col_count), :] * panel_width
    cols = ids[pl.ds(col_count, col_count), :]
    even = lax.broadcasted_iota(jnp.int32, cols.shape, 1) % 2 == 0
    crossed = jnp.where(even, pltpu.roll(cols, LANES - 1, 1), pltpu.roll(cols, 1, 1))
    for cross, columns in enumerate([cols, crossed]):
        target = rows + columns
        found = jnp.full_like(target, kept_count)
        for q in range(kept_count):
            found = jnp.where(target == keep[q], q, found)
        places[pl.ds(cross * col_count, col_count), :] = found
    to_table = pltpu.make_async_copy(places, table, sem.at[1])
    to_table.start()
    total[...] = jnp.zeros_like(total)
    to_table.wait()

    def look(half_panel, counts):
        member = half_panel // halves
        source = (half_panel % halves) * row_count + (member + j - i + row_count) % row_count
        a_near = (member % SIDE == i % SIDE) | (member // SIDE == i // SIDE)
        apart = jnp.abs(j // CORES - source // CORES)
        below = (j // CORES - source // CORES + chips) % chips == 1
        b_near = ((apart <= 1) | (apart == chips - 1)) & ~(below & (j % CORES != source % CORES))

        def scan(into, n):
            for slot in range(b_slots):
                for cross in range(2):
                    q = table[cross * col_count + half_panel, slot]
                    into[n] = (q << 20) | ((half_panel * b_slots + slot) << 10) | (source * b_slots + (slot ^ cross))
                    n = n + (q < kept_count).astype(jnp.int32)
            return n

        return lax.cond(
            a_near & b_near,
            lambda near, far: (scan(listed, near), far),
            lambda near, far: (near, scan(plan, far)),
            *counts,
        )

    near, far = lax.fori_loop(0, col_count, look, (jnp.int32(0), jnp.int32(0)))
    for extra in range(UNROLL):
        listed[near + extra] = kept_count << 20
        plan[far + extra] = kept_count << 20
    plan[layout.count], plan[layout.i], plan[layout.j] = far, i, j
    for q in range(kept_count):
        plan[layout.pos + q] = pos[q]

    def clear(s, carry):
        plan[layout.source + s] = -1
        return carry

    lax.fori_loop(0, capacity + 1, clear, 0, unroll=5)
    to_slot_table.wait()

    def mark(d, carry):
        for m in range(SCAP):
            plan[layout.source + slot_table[d, m]] = d * SCAP + m
        return carry

    lax.fori_loop(0, row_count * col_count, mark, 0, unroll=8)
    bringer.wait()
    multiply_listed(listed, near, a_ref, b_ref, total)


def first_products(sizes, keep, pos, where, exchange, pieces):
    row_count, col_count, b_slots = sizes
    block, kept_count = pieces[0].shape[-1], keep.shape[0]
    rows = col_count * b_slots * block
    return pl.pallas_call(
        functools.partial(first_kernel, sizes, len(pieces)),
        out_shape=[
            pltpu.VMEM((rows, block), jnp.bfloat16),
            pltpu.VMEM((rows, block), jnp.bfloat16),
            pltpu.VMEM((kept_count + 1, block, block), jnp.float32),
            jax.ShapeDtypeStruct((Layout(row_count, col_count, b_slots, kept_count).size,), jnp.int32),
        ],
        in_specs=[SMEM] * 3 + [VMEM] + [ANY] * len(pieces),
        out_specs=[VMEM] * 3 + [SMEM],
        scratch_shapes=[
            pltpu.VMEM((2 * col_count, LANES), jnp.int32),
            pltpu.VMEM((2 * col_count, LANES), jnp.int32),
            pltpu.SMEM((2 * col_count, LANES), jnp.int32),
            pltpu.VMEM((row_count * col_count, LANES), jnp.int32),
            pltpu.SMEM((row_count * col_count, LANES), jnp.int32),
            pltpu.SMEM((2 * col_count * b_slots + UNROLL,), jnp.int32),
            pltpu.SemaphoreType.DMA((len(pieces),)),
            pltpu.SemaphoreType.DMA((2,)),
        ],
        compiler_params=limit(26),
        cost_estimate=pl.CostEstimate(flops=1, bytes_accessed=0, transcendentals=0),
        name="first_products",
    )(keep, pos, where, exchange, *pieces)


def rest_kernel(sizes, parts, plan, *refs):
    row_count, col_count, b_slots = sizes
    pieces, refs = refs[3:3 + parts], refs[3 + parts:]
    a_ref, b_ref, total, send_ref, kept, sems, sem = refs
    kept_count = kept.shape[0]
    layout = Layout(row_count, col_count, b_slots, kept_count)
    bringer = Bringer(a_ref, b_ref, sems, row_count, col_count)
    bring_rest(bringer, pieces, plan[layout.i], plan[layout.j], row_count, col_count)
    bringer.wait()
    multiply_listed(plan, plan[layout.count], a_ref, b_ref, total)

    def finish(q, carry):
        kept[q] = total[q].astype(jnp.bfloat16)
        pltpu.make_async_copy(kept.at[q], send_ref.at[plan[layout.pos + q]], sem).start()
        return carry

    lax.fori_loop(0, kept_count, finish, 0, unroll=2)
    pltpu.make_async_copy(kept, kept, sem).wait()


def rest_products(sizes, kept_count, plan, buffers, pieces):
    row_count, col_count = sizes[:2]
    block = pieces[0].shape[-1]
    return pl.pallas_call(
        functools.partial(rest_kernel, sizes, len(pieces)),
        out_shape=[pltpu.VMEM(b.shape, b.dtype) for b in buffers]
        + [pltpu.HBM((SCAP * row_count * col_count, block, block), jnp.bfloat16)],
        in_specs=[SMEM] + [VMEM] * 3 + [ANY] * len(pieces),
        out_specs=[VMEM] * 3 + [HBM],
        scratch_shapes=[
            pltpu.VMEM((kept_count, block, block), jnp.bfloat16),
            pltpu.SemaphoreType.DMA((len(pieces),)),
            pltpu.SemaphoreType.DMA,
        ],
        input_output_aliases={1 + n: n for n in range(3)},
        compiler_params=limit(28),
        name="rest_products",
    )(plan, *buffers, *pieces)[-1]


def place_kernel(layout, plan, recv_ref, out_ref, zero, sem):
    zero[...] = jnp.zeros_like(zero)

    def place(s, carry):
        r = plan[layout.source + s]

        @pl.when(r >= 0)
        def _():
            pltpu.make_async_copy(recv_ref.at[r], out_ref.at[s], sem).start()

        @pl.when(r < 0)
        def _():
            pltpu.make_async_copy(zero, out_ref.at[s], sem).start()

        return carry

    lax.fori_loop(0, out_ref.shape[0], place, 0, unroll=4)
    pltpu.make_async_copy(recv_ref, out_ref, sem).wait()


def place(layout, plan, recv):
    block = recv.shape[-1]
    return pl.pallas_call(
        functools.partial(place_kernel, layout),
        out_shape=jax.ShapeDtypeStruct(recv.shape, recv.dtype),
        in_specs=[SMEM, VMEM],
        out_specs=HBM,
        scratch_shapes=[pltpu.VMEM((block, block), jnp.bfloat16), pltpu.SemaphoreType.DMA],
        compiler_params=limit(12),
        name="place",
    )(plan, recv)


def gathered(a_own, b_own, b_copy, row_count, col_count, where, outgoing, multiply_near):
    chips, shifts = col_count // CORES, range(1, row_count // SIDE)

    def moved(piece, target):
        pairs = [(d, c, target(d, c)) for d in range(row_count) for c in range(col_count)]
        return lax.ppermute(
            piece, ("row", "col"), [(d * col_count + c, to[0] * col_count + to[1]) for d, c, to in pairs]
        )

    def around(d, c, by, other=False):
        core = CORES - 1 - c % CORES if other else c % CORES
        return d, (c // CORES + by) % chips * CORES + core

    def along(d, c, shift):
        return (d + shift * SIDE) % row_count, c

    def swapped(piece):
        return moved(piece, lambda d, c: around(d, c, 0, True))

    below = [moved(b_copy, lambda d, c: around(d, c, 1))]
    above = [moved(b_own, lambda d, c: around(d, c, -1))]
    beside = moved(a_own, lambda d, c: (d ^ 1, c))
    ahead = [moved(a_own, lambda d, c, shift=shift: along(d, c, shift)) for shift in shifts]
    exchange = lax.all_to_all(outgoing, ("col", "row"), split_axis=0, concat_axis=0, tiled=True)
    above[0] = tied(above[0], *ahead)
    for _ in range(2, chips // 2):
        below.append(moved(below[-1], lambda d, c: around(d, c, 1)))
        above.append(moved(above[-1], lambda d, c: around(d, c, -1)))
    crossing = choose(where, [(piece, beside) for piece in ahead], [1] * len(ahead), exchange)
    opposite = moved(above[-1], lambda d, c: around(d, c, -1))
    diagonal = [
        moved(piece, lambda d, c, shift=shift: (d ^ 1, c) if c % CORES == 0 else along(d, c, shift))
        for shift, piece in zip(shifts, crossing)
    ]

    near = [a_own, beside, *ahead]
    for piece in (b_own, above[0]):
        near += [piece, swapped(piece)]
    near.append(below[0])
    *buffers, plan = multiply_near(exchange, near)
    opposite = list(cut(tied(opposite, plan)))
    crossed = [swapped(opposite[0])]
    opposite[1] = tied(opposite[1], crossed[0])
    crossed.append(swapped(opposite[1]))
    far = list(diagonal)
    for n in range(1, chips // 2 - 1):
        far += [below[n], swapped(below[n]), above[n], swapped(above[n])]
    return buffers, plan, far + [swapped(below[0])] + opposite + crossed


def body(a_blocks, a_rows, b_blocks, b_cols, c_keep, c_owner, c_slot):
    row_count = lax.axis_size("row")
    col_count = lax.axis_size("col")
    block = a_blocks.shape[-1]
    keep, owner_ids, slot_ids = c_keep[0, 0], c_owner[0, 0], c_slot[0, 0]
    sizes = (row_count, col_count, b_cols.shape[1])
    where = jnp.stack([lax.axis_index("row"), lax.axis_index("col")]).astype(jnp.int32)

    b_own = b_blocks[0].reshape(-1, block)
    outgoing, b_copy, pos = announce(row_count, col_count, owner_ids, slot_ids, a_rows, b_cols, b_own)

    buffers, plan, far = gathered(
        a_blocks[0].reshape(-1, block),
        b_own,
        b_copy,
        row_count,
        col_count,
        where,
        outgoing,
        functools.partial(first_products, sizes, keep, pos, where),
    )
    send = rest_products(sizes, keep.shape[0], plan, buffers, far)
    recv = lax.all_to_all(send, ("col", "row"), split_axis=0, concat_axis=0, tiled=True)
    return place(Layout(*sizes, keep.shape[0]), plan, recv)[None]


def solution(mesh):
    return jax.shard_map(
        body,
        mesh=mesh,
        in_specs=(
            P("col", "row", None, None),
            P("col", "row"),
            P("row", "col", None, None),
            P("row", "col"),
            P("row", "col", None),
            P("row", "col", None),
            P("row", "col", None),
        ),
        out_specs=P("row", "col", None, None),
        check_vma=False,
    )
```

```python
import functools

import jax
import jax.numpy as jnp
from jax import lax
from jax.experimental import pallas as pl
from jax.experimental.pallas import tpu as pltpu
from jax.sharding import PartitionSpec as P

RB = 8
SCAP = 2
UNROLL = 8
CORES = 2
SIDE = 2
PARTS = 2
EXCHANGE_ROWS = 8
LANES = 128

SMEM = pl.BlockSpec(memory_space=pltpu.SMEM)
VMEM = pl.BlockSpec(memory_space=pltpu.VMEM)
HBM = pl.BlockSpec(memory_space=pltpu.HBM)
ANY = pl.BlockSpec(memory_space=pl.ANY)


def limit(megabytes):
    return pltpu.CompilerParams(vmem_limit_bytes=megabytes * 1024 * 1024)


def by_column(device, row_count, col_count):
    return device % col_count * row_count + device // col_count


def announce_kernel(row_count, col_count, told, ids, out_ref, pos, base, sent):
    kept_count = pos.shape[0]
    base[...] = jnp.zeros_like(base)
    base[pl.ds(0, 1), :] = jnp.full((1, LANES), SCAP * out_ref.shape[0], jnp.int32)
    base[pl.ds(1, 1), pl.ds(0, ids.shape[1])] = ids[...]
    out_ref[...] = jnp.broadcast_to(base[...][None], out_ref.shape)
    lane = lax.broadcasted_iota(jnp.int32, (1, LANES), 1)

    def clear(d, carry):
        sent[d] = 0
        return carry

    lax.fori_loop(0, out_ref.shape[0], clear, 0, unroll=8)

    def tell(q, carry):
        owner = told[q]
        order = sent[owner]
        pos[q] = by_column(owner, row_count, col_count) * SCAP + order
        sent[owner] = order + 1
        place = by_column(owner, row_count, col_count)
        out_ref[place, pl.ds(0, 1), :] = jnp.where(lane == order, told[kept_count + q], out_ref[place, pl.ds(0, 1), :])
        return carry

    lax.fori_loop(0, kept_count, tell, 0)


def announce(row_count, col_count, owners, slots, a_ids, b_ids):
    return pl.pallas_call(
        functools.partial(announce_kernel, row_count, col_count),
        out_shape=[
            pltpu.VMEM((row_count * col_count, EXCHANGE_ROWS, LANES), jnp.int32),
            jax.ShapeDtypeStruct(owners.shape, jnp.int32),
        ],
        in_specs=[SMEM, VMEM],
        out_specs=[VMEM, SMEM],
        scratch_shapes=[pltpu.VMEM((EXCHANGE_ROWS, LANES), jnp.int32), pltpu.SMEM((row_count * col_count,), jnp.int32)],
        compiler_params=limit(2),
        name="announce",
    )(jnp.concatenate([owners, slots]), jnp.concatenate([a_ids, b_ids], axis=1))


def choose_kernel(cuts, where, *refs):
    count = len(cuts)
    pairs = [(refs[2 * n], refs[2 * n + 1]) for n in range(count)]
    out_refs, sems = list(refs[2 * count + 1:-1]), refs[-1]
    core = where[1] % CORES
    waits = []
    for (first, second), parts in zip(pairs, cuts):
        size = first.shape[0] // parts
        for part in range(parts):
            out, sem, rows = out_refs[len(waits)], sems.at[len(waits)], pl.ds(part * size, size)
            pl.when(core == 0)(pltpu.make_async_copy(first.at[rows], out, sem).start)
            pl.when(core != 0)(pltpu.make_async_copy(second.at[rows], out, sem).start)
            waits.append(pltpu.make_async_copy(first.at[rows], out, sem))
    for copy in waits:
        copy.wait()


def choose(where, pairs, cuts, after):
    shapes = [
        pltpu.VMEM((first.shape[0] // parts, first.shape[1]), first.dtype)
        for (first, _), parts in zip(pairs, cuts)
        for _ in range(parts)
    ]
    return pl.pallas_call(
        functools.partial(choose_kernel, cuts),
        out_shape=shapes,
        in_specs=[SMEM] + [ANY] * (2 * len(pairs) + 1),
        out_specs=[VMEM] * len(shapes),
        scratch_shapes=[pltpu.SemaphoreType.DMA((len(shapes),))],
        compiler_params=limit(8),
        name="choose",
    )(where, *(piece for pair in pairs for piece in pair), after)


def cut_kernel(piece, *refs):
    out_refs, sems = refs[:-1], refs[-1]
    size = out_refs[0].shape[0]
    copies = [pltpu.make_async_copy(piece.at[pl.ds(n * size, size)], out, sems.at[n]) for n, out in enumerate(out_refs)]
    for copy in copies:
        copy.start()
    for copy in copies:
        copy.wait()


def cut(piece):
    part = pltpu.VMEM((piece.shape[0] // PARTS, piece.shape[1]), piece.dtype)
    return pl.pallas_call(
        cut_kernel,
        out_shape=[part] * PARTS,
        in_specs=[ANY],
        out_specs=[VMEM] * PARTS,
        scratch_shapes=[pltpu.SemaphoreType.DMA((PARTS,))],
        compiler_params=limit(2),
        name="cut",
    )(piece)


def tie_kernel(*refs):
    pass


def tied(array, after):
    return pl.pallas_call(
        tie_kernel,
        out_shape=jax.ShapeDtypeStruct(array.shape, array.dtype),
        in_specs=[ANY] * 2,
        out_specs=ANY,
        input_output_aliases={0: 0},
        compiler_params=limit(1),
        name="tied",
    )(array, after)


class Bringer:
    def __init__(self, a_ref, b_ref, sems, row_count, col_count):
        self.refs = {"a": (a_ref, a_ref.shape[0] // row_count), "b": (b_ref, b_ref.shape[0] // col_count)}
        self.sems, self.copies = sems, []

    def bring(self, which, ref, member, part=0, parts=1):
        target, size = self.refs[which]
        size //= parts
        rows = target.at[pl.ds(pl.multiple_of((member * parts + part) * size, size), size)]
        self.copies.append(pltpu.make_async_copy(ref, rows, self.sems.at[len(self.copies)]))
        self.copies[-1].start()

    def wait(self):
        for copy in self.copies:
            copy.wait()


def bring_chip(bringer, refs, shift, j, chips, parts=1):
    z, core = j // CORES, j % CORES
    for ref_core in (core, CORES - 1 - core):
        for part in range(parts):
            bringer.bring("b", refs.pop(0), (z - shift + chips) % chips * CORES + ref_core, part, parts)


def bring_first(bringer, refs, i, j, row_count, col_count):
    refs = list(refs)
    y_count, chips = row_count // SIDE, col_count // CORES
    y, x = i // SIDE, i % SIDE
    bringer.bring("a", refs.pop(0), i)
    bringer.bring("a", refs.pop(0), y * SIDE + SIDE - 1 - x)
    for shift in range(1, y_count):
        bringer.bring("a", refs.pop(0), (y - shift + y_count) % y_count * SIDE + x)
    for shift in (0, chips - 1):
        bring_chip(bringer, refs, shift, j, chips)


def bring_rest(bringer, refs, i, j, row_count, col_count):
    refs = list(refs)
    y_count, chips = row_count // SIDE, col_count // CORES
    y, x = i // SIDE, i % SIDE
    for shift in range(1, y_count):
        bringer.bring("a", refs.pop(0), (y - shift + y_count) % y_count * SIDE + SIDE - 1 - x)
    for shift in range(2, chips // 2):
        bring_chip(bringer, refs, shift, j, chips)
        bring_chip(bringer, refs, chips - shift, j, chips)
    bring_chip(bringer, refs, 1, j, chips)
    bring_chip(bringer, refs, chips // 2, j, chips, PARTS)


class Layout:
    def __init__(self, row_count, col_count, b_slots, kept_count):
        self.count = 2 * col_count * b_slots + UNROLL
        self.i, self.j = self.count + 1, self.count + 2
        self.pos = self.count + 3
        self.source = self.pos + kept_count
        self.size = self.source + SCAP * row_count * col_count + 1


def multiply_listed(listed, count, a_ref, b_ref, total):
    block = a_ref.shape[-1]

    def block_of(ref, index):
        return ref[pl.ds(pl.multiple_of(index * block, block), block), :]

    def multiply(step, carry):
        entries = [listed[step * UNROLL + u] for u in range(UNROLL)]
        products = [
            jnp.dot(
                block_of(a_ref, (entry >> 10) & 1023),
                block_of(b_ref, entry & 1023),
                preferred_element_type=jnp.float32,
            )
            for entry in entries
        ]
        for entry, product in zip(entries, products):
            q = entry >> 20
            total[q] = total[q] + product
        return carry

    lax.fori_loop(0, (count + UNROLL - 1) // UNROLL, multiply, 0)


def first_kernel(sizes, parts, keep, pos, where, exchange, *refs):
    row_count, col_count, b_slots = sizes
    pieces, refs = refs[:parts], refs[parts:]
    a_ref, b_ref, total, plan, ids, places, table, slot_rows, slot_table, listed, sems, sem = refs
    i, j = where[0], where[1]
    kept_count = keep.shape[0]
    panel_width = RB * col_count // row_count
    chips = col_count // CORES
    capacity = SCAP * row_count * col_count
    layout = Layout(row_count, col_count, b_slots, kept_count)
    bringer = Bringer(a_ref, b_ref, sems, row_count, col_count)
    bring_first(bringer, pieces, i, j, row_count, col_count)

    slot_rows[...] = exchange[:, 0, :]
    to_slot_table = pltpu.make_async_copy(slot_rows, slot_table, sem.at[0])
    to_slot_table.start()

    halves = col_count // row_count
    for half_panel in range(col_count):
        member, half = half_panel // halves, half_panel % halves
        rows = exchange[j * row_count + member, pl.ds(1, 1), :]
        ids[pl.ds(half_panel, 1), :] = rows if half == 0 else pltpu.roll(rows, LANES - half * b_slots, 1)
        source = half * row_count + (member + j - i + row_count) % row_count
        cols = exchange[source * row_count + i, pl.ds(1, 1), :]
        ids[pl.ds(col_count + half_panel, 1), :] = pltpu.roll(cols, LANES - halves * b_slots, 1)
    rows = ids[pl.ds(0, col_count), :] * panel_width
    cols = ids[pl.ds(col_count, col_count), :]
    even = lax.broadcasted_iota(jnp.int32, cols.shape, 1) % 2 == 0
    crossed = jnp.where(even, pltpu.roll(cols, LANES - 1, 1), pltpu.roll(cols, 1, 1))
    for cross, columns in enumerate([cols, crossed]):
        target = rows + columns
        found = jnp.full_like(target, kept_count)
        for q in range(kept_count):
            found = jnp.where(target == keep[q], q, found)
        places[pl.ds(cross * col_count, col_count), :] = found
    to_table = pltpu.make_async_copy(places, table, sem.at[1])
    to_table.start()
    total[...] = jnp.zeros_like(total)
    to_table.wait()

    def look(half_panel, counts):
        member = half_panel // halves
        source = (half_panel % halves) * row_count + (member + j - i + row_count) % row_count
        a_near = (member % SIDE == i % SIDE) | (member // SIDE == i // SIDE)
        b_near = (source // CORES - j // CORES + chips) % chips <= 1

        def scan(into, n):
            for slot in range(b_slots):
                for cross in range(2):
                    q = table[cross * col_count + half_panel, slot]
                    into[n] = (q << 20) | ((half_panel * b_slots + slot) << 10) | (source * b_slots + (slot ^ cross))
                    n = n + (q < kept_count).astype(jnp.int32)
            return n

        return lax.cond(
            a_near & b_near,
            lambda near, far: (scan(listed, near), far),
            lambda near, far: (near, scan(plan, far)),
            *counts,
        )

    near, far = lax.fori_loop(0, col_count, look, (jnp.int32(0), jnp.int32(0)))
    for extra in range(UNROLL):
        listed[near + extra] = kept_count << 20
        plan[far + extra] = kept_count << 20
    plan[layout.count], plan[layout.i], plan[layout.j] = far, i, j
    for q in range(kept_count):
        plan[layout.pos + q] = pos[q]

    def clear(s, carry):
        plan[layout.source + s] = -1
        return carry

    lax.fori_loop(0, capacity + 1, clear, 0, unroll=5)
    to_slot_table.wait()

    def mark(d, carry):
        for m in range(SCAP):
            plan[layout.source + slot_table[d, m]] = d * SCAP + m
        return carry

    lax.fori_loop(0, row_count * col_count, mark, 0, unroll=8)
    bringer.wait()
    multiply_listed(listed, near, a_ref, b_ref, total)


def first_products(sizes, keep, pos, where, exchange, pieces):
    row_count, col_count, b_slots = sizes
    block, kept_count = pieces[0].shape[-1], keep.shape[0]
    rows = col_count * b_slots * block
    return pl.pallas_call(
        functools.partial(first_kernel, sizes, len(pieces)),
        out_shape=[
            pltpu.VMEM((rows, block), jnp.bfloat16),
            pltpu.VMEM((rows, block), jnp.bfloat16),
            pltpu.VMEM((kept_count + 1, block, block), jnp.float32),
            jax.ShapeDtypeStruct((Layout(row_count, col_count, b_slots, kept_count).size,), jnp.int32),
        ],
        in_specs=[SMEM] * 3 + [VMEM] + [ANY] * len(pieces),
        out_specs=[VMEM] * 3 + [SMEM],
        scratch_shapes=[
            pltpu.VMEM((2 * col_count, LANES), jnp.int32),
            pltpu.VMEM((2 * col_count, LANES), jnp.int32),
            pltpu.SMEM((2 * col_count, LANES), jnp.int32),
            pltpu.VMEM((row_count * col_count, LANES), jnp.int32),
            pltpu.SMEM((row_count * col_count, LANES), jnp.int32),
            pltpu.SMEM((2 * col_count * b_slots + UNROLL,), jnp.int32),
            pltpu.SemaphoreType.DMA((len(pieces),)),
            pltpu.SemaphoreType.DMA((2,)),
        ],
        compiler_params=limit(26),
        cost_estimate=pl.CostEstimate(flops=1, bytes_accessed=0, transcendentals=0),
        name="first_products",
    )(keep, pos, where, exchange, *pieces)


def rest_kernel(sizes, parts, plan, *refs):
    row_count, col_count, b_slots = sizes
    pieces, refs = refs[3:3 + parts], refs[3 + parts:]
    a_ref, b_ref, total, send_ref, kept, sems, sem = refs
    kept_count = kept.shape[0]
    layout = Layout(row_count, col_count, b_slots, kept_count)
    bringer = Bringer(a_ref, b_ref, sems, row_count, col_count)
    bring_rest(bringer, pieces, plan[layout.i], plan[layout.j], row_count, col_count)
    bringer.wait()
    multiply_listed(plan, plan[layout.count], a_ref, b_ref, total)

    def finish(q, carry):
        kept[q] = total[q].astype(jnp.bfloat16)
        pltpu.make_async_copy(kept.at[q], send_ref.at[plan[layout.pos + q]], sem).start()
        return carry

    lax.fori_loop(0, kept_count, finish, 0, unroll=2)
    pltpu.make_async_copy(kept, kept, sem).wait()


def rest_products(sizes, kept_count, plan, buffers, pieces):
    row_count, col_count = sizes[:2]
    block = pieces[0].shape[-1]
    return pl.pallas_call(
        functools.partial(rest_kernel, sizes, len(pieces)),
        out_shape=[pltpu.VMEM(b.shape, b.dtype) for b in buffers]
        + [pltpu.HBM((SCAP * row_count * col_count, block, block), jnp.bfloat16)],
        in_specs=[SMEM] + [VMEM] * 3 + [ANY] * len(pieces),
        out_specs=[VMEM] * 3 + [HBM],
        scratch_shapes=[
            pltpu.VMEM((kept_count, block, block), jnp.bfloat16),
            pltpu.SemaphoreType.DMA((len(pieces),)),
            pltpu.SemaphoreType.DMA,
        ],
        input_output_aliases={1 + n: n for n in range(3)},
        compiler_params=limit(28),
        name="rest_products",
    )(plan, *buffers, *pieces)[-1]


def place_kernel(layout, plan, recv_ref, out_ref, zero, sem):
    zero[...] = jnp.zeros_like(zero)

    def place(s, carry):
        r = plan[layout.source + s]

        @pl.when(r >= 0)
        def _():
            pltpu.make_async_copy(recv_ref.at[r], out_ref.at[s], sem).start()

        @pl.when(r < 0)
        def _():
            pltpu.make_async_copy(zero, out_ref.at[s], sem).start()

        return carry

    lax.fori_loop(0, out_ref.shape[0], place, 0, unroll=4)
    pltpu.make_async_copy(recv_ref, out_ref, sem).wait()


def place(layout, plan, recv):
    block = recv.shape[-1]
    return pl.pallas_call(
        functools.partial(place_kernel, layout),
        out_shape=jax.ShapeDtypeStruct(recv.shape, recv.dtype),
        in_specs=[SMEM, VMEM],
        out_specs=HBM,
        scratch_shapes=[pltpu.VMEM((block, block), jnp.bfloat16), pltpu.SemaphoreType.DMA],
        compiler_params=limit(12),
        name="place",
    )(plan, recv)


def gathered(a_own, b_own, row_count, col_count, where, outgoing, multiply_near):
    chips, shifts = col_count // CORES, range(1, row_count // SIDE)

    def moved(piece, target):
        pairs = [(d, c, target(d, c)) for d in range(row_count) for c in range(col_count)]
        return lax.ppermute(
            piece, ("row", "col"), [(d * col_count + c, to[0] * col_count + to[1]) for d, c, to in pairs]
        )

    def around(d, c, by, other=False):
        core = CORES - 1 - c % CORES if other else c % CORES
        return d, (c // CORES + by) % chips * CORES + core

    def along(d, c, shift):
        return (d + shift * SIDE) % row_count, c

    def swapped(piece):
        return moved(piece, lambda d, c: around(d, c, 0, True))

    below = [moved(b_own, lambda d, c: around(d, c, 1))]
    above = [moved(b_own, lambda d, c: around(d, c, -1))]
    beside = moved(a_own, lambda d, c: (d ^ 1, c))
    ahead = [moved(a_own, lambda d, c, shift=shift: along(d, c, shift)) for shift in shifts]
    exchange = lax.all_to_all(outgoing, ("col", "row"), split_axis=0, concat_axis=0, tiled=True)
    for _ in range(2, chips // 2):
        below.append(moved(below[-1], lambda d, c: around(d, c, 1)))
        above.append(moved(above[-1], lambda d, c: around(d, c, -1)))
    crossing = choose(where, [(piece, beside) for piece in ahead], [1] * len(ahead), exchange)
    opposite = moved(above[-1], lambda d, c: around(d, c, -1))
    diagonal = [
        moved(piece, lambda d, c, shift=shift: (d ^ 1, c) if c % CORES == 0 else along(d, c, shift))
        for shift, piece in zip(shifts, crossing)
    ]

    near = [a_own, beside, *ahead]
    for piece in (b_own, above[0]):
        near += [piece, swapped(piece)]
    *buffers, plan = multiply_near(exchange, near)
    opposite = list(cut(tied(opposite, plan)))
    crossed = [swapped(opposite[0])]
    opposite[1] = tied(opposite[1], crossed[0])
    crossed.append(swapped(opposite[1]))
    far = list(diagonal)
    for n in range(1, chips // 2 - 1):
        far += [below[n], swapped(below[n]), above[n], swapped(above[n])]
    return buffers, plan, far + [below[0], swapped(below[0])] + opposite + crossed


def body(a_blocks, a_rows, b_blocks, b_cols, c_keep, c_owner, c_slot):
    row_count = lax.axis_size("row")
    col_count = lax.axis_size("col")
    block = a_blocks.shape[-1]
    keep, owner_ids, slot_ids = c_keep[0, 0], c_owner[0, 0], c_slot[0, 0]
    sizes = (row_count, col_count, b_cols.shape[1])
    where = jnp.stack([lax.axis_index("row"), lax.axis_index("col")]).astype(jnp.int32)

    b_own = b_blocks[0].reshape(-1, block)
    outgoing, pos = announce(row_count, col_count, owner_ids, slot_ids, a_rows, b_cols)

    buffers, plan, far = gathered(
        a_blocks[0].reshape(-1, block),
        b_own,
        row_count,
        col_count,
        where,
        outgoing,
        functools.partial(first_products, sizes, keep, pos, where),
    )
    send = rest_products(sizes, keep.shape[0], plan, buffers, far)
    recv = lax.all_to_all(send, ("col", "row"), split_axis=0, concat_axis=0, tiled=True)
    return place(Layout(*sizes, keep.shape[0]), plan, recv)[None]


def solution(mesh):
    return jax.shard_map(
        body,
        mesh=mesh,
        in_specs=(
            P("col", "row", None, None),
            P("col", "row"),
            P("row", "col", None, None),
            P("row", "col"),
            P("row", "col", None),
            P("row", "col", None),
            P("row", "col", None),
        ),
        out_specs=P("row", "col", None, None),
        check_vma=False,
    )
```
